32 devices in a mesh: groups: 2 (over y), row: 16 (over z, x, core).
Axes of the slice: x: 2, y: 2, z: 4, core: 2. Of those that a mesh axis runs over, the one named last changes fastest.
Arguments:
- frontal: float32 [16384, 8192], P(('groups', 'row')), parts along dimension 0, may hold values from -8 to 192, as said below
- child_tiles: bfloat16 [2048, 128, 128], P(('groups', 'row')), parts along dimension 0, may hold values from -3 to 3
- child_rows: int32 [2048, 1], P(('groups', 'row')), parts along dimension 0, may hold values from 0 to 63; in each aligned block of 64 rows (0 to 63, 64 to 127, ...) at most 2 rows name the same one
- child_cols: int32 [2048], P(('groups', 'row')), parts along dimension 0, may hold values from 0 to 63
Outputs:
- factored: float32 [16384, 8192], P(('groups', 'row')), parts along dimension 0
The draws below stay inside these ranges and needn't reach their ends.
There are 2 independent parts, one for each index of `groups`. The reference program is written for one: setup_inputs(seed, part) draws one part's arguments, and reference() takes and returns one part's arrays. A program takes and returns all parts, laid end to end along the dimension named above; each array names one. Nothing has to cross between parts.
Inputs may be any that keep to these rules, and one draw needn't show every extreme that they name: `frontal`: the leading square block of 256 rows and columns is symmetric and strongly diagonally dominant, so that it stays positive definite after the child tiles are added. `child_rows`: among the 64 tiles of one device no parent tile row is named by more than 2 of them; in every draw some device names some parent tile row exactly 2 times.
All inputs are finite; a program needn't handle non-finite values.
Results may differ from the reference program's by a relative error of at most 0.0003.
Values may be sent and summed in bfloat16 or wider, within the bound.
No kernel may reach another device: no remote copies, remote signals or barrier semaphores. Data moves between devices by JAX's collectives and lax.ppermute only.
A program may use at most 192 MiB of HBM per device.

```python
import math
import jax
import jax.numpy as jnp
import numpy as np
from jax import lax

FRONT_ORDER = 8192
TILE_SIDE = 128
TILES_DEV = 64
TILE_ROWS = 64
MOST_SAME = 2
CHILD_TILES = 1024


def draw_frontal(key, part):
    key = jax.random.fold_in(key, 11)
    first_key, second_key, third_key = jax.random.split(key, 3)
    leading = 2 * TILE_SIDE
    row_ids = jnp.arange(FRONT_ORDER)[:, None]
    col_ids = jnp.arange(FRONT_ORDER)[None, :]
    base = jnp.clip(jax.random.normal(first_key, (FRONT_ORDER, FRONT_ORDER), jnp.float32), -4.0, 4.0)
    base = base * jnp.where((row_ids >= leading) & (col_ids < leading), 2.0, 1.0)
    noise = jax.random.uniform(second_key, (leading, leading), jnp.float32, -0.25, 0.25)
    mirror = 0.5 * (noise + noise.T)
    heights = TILE_SIDE * (1.25 + 0.25 * jax.random.uniform(third_key, (leading,), jnp.float32))
    identity = jnp.eye(leading, dtype=jnp.float32)
    corner = mirror * (1.0 - identity) + identity * heights[None, :]
    return base.at[:leading, :leading].set(corner)


def set_ends(result, key, least, high):
    shape = result.shape
    place = [jax.random.randint(jax.random.fold_in(key, axis), (), 0, shape[axis]) for axis in range(len(shape))]
    result = result.at[tuple(place)].set(least)
    longest = shape.index(max(shape))
    place[longest] = (place[longest] + 1) % shape[longest]
    return result.at[tuple(place)].set(high)


def shard_levels(key, shape, cuts, least, high):
    loudness, own = 1.0, jax.random.fold_in(key, 6)
    for dim, shards_of in cuts:
        steps = jnp.exp(jax.random.uniform(jax.random.fold_in(own, dim), (shards_of,), jnp.float32, least / len(cuts), high / len(cuts)))
        loudness = loudness * jnp.repeat(steps, shape[dim] // shards_of).reshape([-1 if axis == dim else 1 for axis in range(len(shape))])
    return loudness


def deal_out(key, own, number, rows, count, top, most, skew):
    ranking = jax.random.permutation(key, count)
    heavy_load, common = load_shares(count, rows * top, most, skew, True), load_shares(count, rows * top, most, skew, False)
    places = jnp.arange(count)

    def named(sizes, rotation):
        used = int((sizes > 0).sum())
        fixed = max(1, used // 4)
        shifted = fixed + (places - fixed + rotation * (used - fixed)) % max(1, count - fixed)
        return jnp.zeros((count,), jnp.int32).at[ranking[jnp.where(places < fixed, places, shifted)]].set(jnp.asarray(sizes, jnp.int32))

    sizes = jnp.where(number % 4 == 0, named(heavy_load, number // 4), named(common, number - number // 4 - 1))
    mixed = jax.random.permutation(jax.random.fold_in(own, 3), count)
    giver, receiver = mixed[0:count // 2 * 2:2], mixed[1:count // 2 * 2:2]
    room = jnp.minimum(sizes[giver] - 1, most - sizes[receiver]) // 2
    room = jnp.where((giver == ranking[0]) | (receiver == ranking[0]) | (sizes[receiver] == 0), 0, jnp.maximum(room, 0))
    shifted = jax.random.randint(jax.random.fold_in(own, 4), (count // 2,), 0, 1 << 20) % (room + 1)
    sizes = sizes.at[giver].add(-shifted).at[receiver].add(shifted)
    members = jnp.searchsorted(jnp.cumsum(sizes), jnp.arange(rows * top), side="right").astype(jnp.int32)
    table = members.reshape(top, rows).T
    table = table[jax.random.permutation(jax.random.fold_in(own, 1), rows)]
    rotation = jax.random.randint(jax.random.fold_in(own, 2), (rows, 1), 0, top)
    return jnp.take_along_axis(table, (jnp.arange(top)[None, :] + rotation) % top, axis=1)


def load_shares(amount, total, most, skew, full):
    weights = [(1 << 20) // math.isqrt(rank ** skew) + 1 for rank in range(1, amount + 1)]
    largest = most if full else min(most, max(-(-total // amount), total * weights[0] // sum(weights)))
    least = 1 if total - largest >= amount - 1 else 0
    counts, rest = [largest] + [least] * (amount - 1), total - largest - least * (amount - 1)
    while rest > 0:
        candidates = [i for i in range(1, amount) if counts[i] < largest] or [i for i in range(1, amount) if counts[i] < most]
        whole, left = sum([weights[i] for i in candidates]), rest
        for i in candidates:
            addition = min(most - counts[i], max(1, left * weights[i] // whole), rest)
            counts[i] = counts[i] + addition
            rest = rest - addition
    return np.array(counts)


def bell_draw(rng, extent, deviation, bound, cuts=(), kind=jnp.bfloat16):
    values = deviation * jax.random.normal(rng, extent, jnp.float32)
    if cuts:
        values = values * shard_levels(rng, extent, cuts, -0.22, 0.18)
    return jnp.clip(values, -bound, bound).astype(kind)


def setup_inputs(seed: int = 0, part: int = 0) -> dict:
    streams_of = jax.random.split(jax.random.key(seed), 5)
    own_keys = jax.random.split(jax.random.fold_in(streams_of[4], part), 5)
    frontal = draw_frontal(jax.random.fold_in(jax.random.fold_in(streams_of[4], part), 71), part)
    child_tiles = bell_draw(own_keys[1], (CHILD_TILES, TILE_SIDE, TILE_SIDE), 0.5, 3.0, ((0, 16),))
    child_rows_keys = jax.random.split(jax.random.fold_in(own_keys[2], 1), CHILD_TILES // TILES_DEV)
    child_rows_turns = jax.random.permutation(jax.random.fold_in(own_keys[2], 3), CHILD_TILES // TILES_DEV)
    child_rows = jax.vmap(lambda own, number: deal_out(jax.random.fold_in(own_keys[2], 2), own, number, TILES_DEV, TILE_ROWS, 1, MOST_SAME, 2))(child_rows_keys, child_rows_turns).reshape((CHILD_TILES, 1))
    child_cols = set_ends(jax.random.randint(own_keys[3], (CHILD_TILES,), 0, TILE_ROWS), jax.random.fold_in(own_keys[3], 1), 0, TILE_ROWS - 1).astype(jnp.int32)
    return {"frontal": frontal, "child_tiles": child_tiles, "child_rows": child_rows, "child_cols": child_cols}


highest = lax.Precision.HIGHEST

def factor_rows(column_block, square_block, first_row, low_edge):
    tile_side = square_block.shape[0]
    factor = jnp.linalg.cholesky(square_block)
    identity = jnp.eye(tile_side, dtype=column_block.dtype)
    inverse = jax.scipy.linalg.solve_triangular(factor, identity, lower=True)
    solved = jnp.dot(column_block, inverse.T, precision=highest)
    row_ids = first_row + jnp.arange(column_block.shape[0], dtype=jnp.int32)
    inside = (row_ids >= low_edge) & (row_ids < low_edge + tile_side)
    within = jnp.take(factor, jnp.clip(row_ids - low_edge, 0, tile_side - 1), axis=0)
    before = row_ids < low_edge
    return jnp.where(inside[:, None], within, jnp.where(before[:, None], jnp.zeros_like(solved), solved))

def apply_panel(current, panel_rows, update, low_edge):
    tile_side = panel_rows.shape[1]
    col_ids = jnp.arange(current.shape[1], dtype=jnp.int32)[None, :]
    current = jnp.where(col_ids >= low_edge + tile_side, current - update, current)
    return current.at[:, low_edge:low_edge + tile_side].set(panel_rows)

def reference(frontal, child_tiles, child_rows, child_cols):
    labels = (child_rows[:, 0] * TILE_ROWS + child_cols).astype(jnp.int32)
    summed = jax.ops.segment_sum(child_tiles.astype(jnp.float32), labels, num_segments=TILE_ROWS * TILE_ROWS)
    extend_sum = summed.reshape(TILE_ROWS, TILE_ROWS, TILE_SIDE, TILE_SIDE).transpose(0, 2, 1, 3).reshape(FRONT_ORDER, FRONT_ORDER)
    current = frontal + extend_sum
    for panel_index in range(2):
        low_edge = panel_index * TILE_SIDE
        high_edge = low_edge + TILE_SIDE
        panel_all = factor_rows(current[:, low_edge:high_edge], current[low_edge:high_edge, low_edge:high_edge], 0, low_edge)
        update = jnp.dot(panel_all, panel_all.T, precision=highest)
        current = apply_panel(current, panel_all, update, low_edge)
    return current
```

```python
import functools
import jax
import jax.numpy as jnp
from jax import lax
from jax.experimental import pallas as pl
from jax.experimental.pallas import tpu as pltpu
from jax.sharding import PartitionSpec as P

MOST_SAME = 2
FIRST = 3
SECOND = 3
HEAD = 16
VMEM_LIMIT = 56 << 20


highest = lax.Precision.HIGHEST
f32, f16, bf16 = jnp.float32, jnp.float16, jnp.bfloat16


def loop(count, body):
    lax.fori_loop(0, count, lambda i, carry: (body(i), carry)[1], 0)


def pack_kernel(
    tile_rows, per_dev, rows_ref, cols_ref, tiles_ref, first_ref, second_ref, third_ref,
    heads, heads_out, counts, sems, head_sem,
):
    tiles, side, _ = tiles_ref.shape
    devices = first_ref.shape[0]
    lanes = lax.broadcasted_iota(jnp.int32, (8, 128), 1)
    subs = lax.broadcasted_iota(jnp.int32, (8, 128), 0)
    heads[...] = jnp.zeros_like(heads)

    def clear(d):
        counts[d] = 0

    loop(devices, clear)

    def place(i, wanted):
        row, col = rows_ref[i], cols_ref[i]

        @pl.when((col < 2) == wanted)
        def _():
            d, q = row // per_dev, row % per_dev
            s = counts[d]
            counts[d] = s + 1
            here = (lanes == s) & (subs == 0)
            heads[d] = jnp.where(here, (q * tile_rows + col + 1).astype(f32), heads[d])

            @pl.when(s < FIRST)
            def _():
                pltpu.make_async_copy(
                    tiles_ref.at[i], first_ref.at[d, pl.ds(s * side, side)], sems.at[i]
                ).start()

            @pl.when((s >= FIRST) & (s < FIRST + SECOND))
            def _():
                pltpu.make_async_copy(
                    tiles_ref.at[i], second_ref.at[d, pl.ds((s - FIRST) * side, side)], sems.at[i]
                ).start()

            @pl.when(s >= FIRST + SECOND)
            def _():
                pltpu.make_async_copy(
                    tiles_ref.at[i],
                    third_ref.at[d, pl.ds((s - FIRST - SECOND) * side, side)],
                    sems.at[i],
                ).start()

    def most():
        return lax.fori_loop(0, devices, lambda d, m: jnp.maximum(m, counts[d]), 0)

    loop(tiles, lambda i: place(i, True))
    lead_over = (most() > FIRST).astype(f32)
    loop(tiles, lambda i: place(i, False))
    over = (most() > FIRST + SECOND).astype(f32)
    flags = jnp.where(lanes == 0, lead_over, jnp.where(lanes == 1, over, 0.0))
    marked = jnp.where((subs == 1)[None], flags[None], heads[...])
    heads_out[...] = jnp.concatenate([marked, jnp.zeros_like(marked)], axis=1).astype(bf16)
    copy = pltpu.make_async_copy(heads_out, first_ref.at[:, pl.ds(FIRST * side, HEAD)], head_sem)
    copy.start()

    def finish(i):
        pltpu.make_async_copy(tiles_ref.at[i], first_ref.at[0, pl.ds(0, side)], sems.at[i]).wait()

    loop(tiles, finish)
    copy.wait()


def pack(child_tiles, child_rows, child_cols, devices, tile_rows):
    tiles, side, _ = child_tiles.shape
    per_dev = tile_rows // devices
    third = MOST_SAME * per_dev - FIRST - SECOND
    smem, anyw = (pl.BlockSpec(memory_space=m) for m in (pltpu.SMEM, pl.ANY))
    return pl.pallas_call(
        functools.partial(pack_kernel, tile_rows, per_dev),
        grid=(1,),
        out_shape=(
            jax.ShapeDtypeStruct((devices, FIRST * side + HEAD, side), bf16),
            jax.ShapeDtypeStruct((devices, SECOND * side, side), bf16),
            jax.ShapeDtypeStruct((devices, third * side, side), bf16),
        ),
        in_specs=[smem, smem, pl.BlockSpec((tiles, side, side), lambda i: (0, 0, 0))],
        out_specs=(anyw, anyw, anyw),
        scratch_shapes=[
            pltpu.VMEM((devices, 8, 128), f32),
            pltpu.VMEM((devices, HEAD, 128), bf16),
            pltpu.SMEM((devices,), jnp.int32),
            pltpu.SemaphoreType.DMA((tiles,)),
            pltpu.SemaphoreType.DMA,
        ],
        compiler_params=pltpu.CompilerParams(vmem_limit_bytes=VMEM_LIMIT),
        name="pack",
    )(child_rows[:, 0], child_cols, child_tiles)


def lead_kernel(tile_rows, slots, labels_ref, front_ref, more_ref, tiles_ref, out_ref):
    side = tiles_ref.shape[2]
    out_ref[...] = front_ref[...] + more_ref[...]

    def body(n):
        d, s = n // FIRST, n % FIRST
        label = labels_ref[d * slots + s]
        q, col = label // tile_rows, label % tile_rows

        @pl.when((label >= 0) & (col < 2))
        def _():
            at = (pl.ds(pl.multiple_of(q * side, side), side),
                  pl.ds(pl.multiple_of(col * side, side), side))
            out_ref[at] = out_ref[at] + tiles_ref[d, pl.ds(pl.multiple_of(s * side, side), side)].astype(f32)

    loop(tiles_ref.shape[0] * FIRST, body)


def lead_columns(labels, frontal, more, arrived, tile_rows):
    rows = frontal.shape[0]
    side = arrived.shape[2]
    return pl.pallas_call(
        functools.partial(lead_kernel, tile_rows, labels.shape[1]),
        grid=(1,),
        out_shape=jax.ShapeDtypeStruct((rows, 2 * side), f32),
        in_specs=[
            pl.BlockSpec(memory_space=pltpu.SMEM),
            pl.BlockSpec((rows, 2 * side), lambda i: (0, 0)),
            pl.BlockSpec((rows, 2 * side), lambda i: (0, 0)),
            pl.BlockSpec(arrived.shape, lambda i: (0, 0, 0)),
        ],
        out_specs=pl.BlockSpec((rows, 2 * side), lambda i: (0, 0)),
        compiler_params=pltpu.CompilerParams(vmem_limit_bytes=VMEM_LIMIT),
        name="lead_columns",
    )(labels.reshape(-1), frontal, more, arrived)


def nt_dot(a, b):
    return lax.dot_general(a, b, (((1,), (1,)), ((), ())), preferred_element_type=f32)


def update_kernel(order_ref, front_ref, panel_ref, whi_ref, wlo_ref, hi_ref, lo_ref, out_ref):
    lead = panel_ref.shape[1]
    hi = hi_ref[...]
    update = nt_dot(whi_ref[...], hi) + nt_dot(whi_ref[...], lo_ref[...]) + nt_dot(wlo_ref[...], hi)
    out_ref[...] = front_ref[...] - update

    @pl.when(pl.program_id(0) == 0)
    def _():
        out_ref[:, :lead] = panel_ref[...]


def update(frontal, panel, whi, wlo, hi, lo, order):
    rows, cols = frontal.shape
    lead = panel.shape[1]
    fixed = lambda shape: pl.BlockSpec(shape, lambda j, order: (0, 0))
    return pl.pallas_call(
        update_kernel,
        grid_spec=pltpu.PrefetchScalarGridSpec(
            num_scalar_prefetch=1,
            grid=(cols // rows,),
            in_specs=[
                pl.BlockSpec((rows, rows), lambda j, order: (0, j)),
                fixed((rows, lead)), fixed((rows, lead)), fixed((rows, lead)),
                pl.BlockSpec((rows, lead), lambda j, order: (order[j], 0)),
                pl.BlockSpec((rows, lead), lambda j, order: (order[j], 0)),
            ],
            out_specs=pl.BlockSpec((rows, rows), lambda j, order: (0, j)),
        ),
        out_shape=jax.ShapeDtypeStruct((rows, cols), f32),
        compiler_params=pltpu.CompilerParams(vmem_limit_bytes=VMEM_LIMIT),
        cost_estimate=pl.CostEstimate(flops=6 * rows * cols * lead, bytes_accessed=8 * rows * cols, transcendentals=0),
        name="update",
    )(order, frontal, panel, whi, wlo, hi, lo)


def place_kernel(tile_rows, labels_ref, owner_ref, tiles_ref, front_ref, out_ref, held, listed, in_sems, out_sems):
    side = tiles_ref.shape[2]
    slots = tiles_ref.shape[1] // side

    def spot(n):
        label = labels_ref[n]
        q, col = label // tile_rows, label % tile_rows
        return out_ref.at[pl.ds(pl.multiple_of(q * side, side), side), pl.ds(pl.multiple_of(col * side, side), side)]

    def fetch(n, used):
        listed[used] = n

        @pl.when(owner_ref[n] == n)
        def _():
            pltpu.make_async_copy(spot(n), held.at[n], in_sems.at[n]).start()

        return used + (labels_ref[n] >= 0).astype(jnp.int32)

    def add(i):
        n = listed[i]
        m = owner_ref[n]

        @pl.when(m == n)
        def _():
            pltpu.make_async_copy(spot(n), held.at[n], in_sems.at[n]).wait()

        held[m] += tiles_ref[n // slots, pl.ds(pl.multiple_of(n % slots * side, side), side)].astype(f32)

    def put(i):
        n = listed[i]

        @pl.when(owner_ref[n] == n)
        def _():
            pltpu.make_async_copy(held.at[n], spot(n), out_sems.at[n]).start()

    def finish(i):
        n = listed[i]

        @pl.when(owner_ref[n] == n)
        def _():
            pltpu.make_async_copy(held.at[n], spot(n), out_sems.at[n]).wait()

    used = lax.fori_loop(0, tiles_ref.shape[0] * slots, fetch, 0)
    for step in (add, put, finish):
        loop(used, step)


def place(front, labels, tiles, tile_rows):
    side = tiles.shape[2]
    labels = labels.reshape(-1)
    size = labels.size
    ids = jnp.arange(size, dtype=jnp.int32)
    owner = jnp.min(jnp.where(labels[:, None] == labels[None, :], ids[None, :], size), axis=1)
    owner = jnp.where(labels < 0, -1, owner)
    smem = pl.BlockSpec(memory_space=pltpu.SMEM)
    return pl.pallas_call(
        functools.partial(place_kernel, tile_rows),
        grid=(1,),
        out_shape=jax.ShapeDtypeStruct(front.shape, f32),
        in_specs=[smem, smem, pl.BlockSpec(tiles.shape, lambda i: (0, 0, 0)), pl.BlockSpec(memory_space=pl.ANY)],
        out_specs=pl.BlockSpec(memory_space=pl.ANY),
        input_output_aliases={3: 0},
        scratch_shapes=[
            pltpu.VMEM((size, side, side), f32),
            pltpu.SMEM((size + 1,), jnp.int32),
            pltpu.SemaphoreType.DMA((size,)),
            pltpu.SemaphoreType.DMA((size,)),
        ],
        compiler_params=pltpu.CompilerParams(vmem_limit_bytes=VMEM_LIMIT),
        name="place",
    )(labels, owner, tiles, front)


def bdot(a, b, dims):
    return lax.dot_general(a, b, (dims, ((), ())), precision=highest, preferred_element_type=f32)


STEP = 4


def eliminate(block):
    side = block.shape[0]
    lanes = lax.broadcasted_iota(jnp.int32, (1, side), 1)
    left = block
    right = jnp.where(
        lax.broadcasted_iota(jnp.int32, (side, side), 0) == lax.broadcasted_iota(jnp.int32, (side, side), 1), 1.0, 0.0
    )
    upper_rows, inverse_rows = [], []
    for k in range(0, side, STEP):
        base = k // 8 * 8
        cut = base - (side - left.shape[0])
        left, right = left[cut:], right[cut:]
        height = left.shape[0]
        wide = [jnp.broadcast_to(left[:, k + i : k + i + 1], (height, side)) for i in range(STEP)]
        cols, ups, invs = [], [], []
        for i in range(STEP):
            at = k + i - base
            col, up, inv = wide[i], left[at : at + 1], right[at : at + 1]
            for j in range(i):
                factor = cols[j][at : at + 1]
                col = col - cols[j] * factor
                up = up - ups[j] * factor
                inv = inv - invs[j] * factor
            scale = lax.rsqrt(col[at : at + 1])
            cols.append(col * scale)
            ups.append(up * scale)
            invs.append(inv * scale)
            upper_rows.append(jnp.where(lanes >= k + i, ups[i], 0.0))
            inverse_rows.append(invs[i])
        for i in range(STEP):
            left = left - cols[i] * ups[i]
            right = right - cols[i] * invs[i]
    return jnp.concatenate(upper_rows, axis=0), jnp.concatenate(inverse_rows, axis=0)


def factor_kernel(first_ref, block_ref, columns_ref, panel_ref, whi_ref, wlo_ref):
    lead = block_ref.shape[1]
    side = lead // 2
    eye = lax.broadcasted_iota(jnp.int32, (side, side), 0) == lax.broadcasted_iota(jnp.int32, (side, side), 1)
    b11, b21, b22 = block_ref[:side, :side], block_ref[side:, :side], block_ref[side:, side:]
    one = (b11 + b11.T) * 0.5 + jnp.where(eye, block_ref[0:1, side:], 0.0)
    two = (b22 + b22.T) * 0.5 + jnp.where(eye, block_ref[1:2, side:], 0.0)
    nt, nn = ((1,), (1,)), ((1,), (0,))
    up_one, inv_one = eliminate(one)
    below = bdot(b21, inv_one, nt)
    up_two, inv_two = eliminate(two - bdot(below, below, nt))
    corner = -bdot(inv_two, bdot(below, inv_one, nn), nn)
    left, right = columns_ref[:, :side], columns_ref[:, side:]
    panel_left = bdot(left, inv_one, nt)
    panel_right = bdot(left, corner, nt) + bdot(right, inv_two, nt)
    weight_left = bdot(panel_left, inv_one, nn) + bdot(panel_right, corner, nn)
    weight_right = bdot(panel_right, inv_two, nn)

    def put(rows, cols, panel, weight):
        panel_ref[rows, cols] = panel
        hi = weight.astype(bf16)
        whi_ref[rows, cols] = hi
        wlo_ref[rows, cols] = (weight - hi.astype(f32)).astype(bf16)

    everything, before, after = slice(None), slice(0, side), slice(side, lead)
    put(everything, before, panel_left, weight_left)
    put(everything, after, panel_right, weight_right)

    @pl.when(first_ref[0] == 0)
    def _():
        one_eye, zero = jnp.where(eye, 1.0, 0.0), jnp.zeros((side, side), f32)
        put(before, before, up_one.T, one_eye)
        put(before, after, zero, zero)
        put(after, before, below, zero)
        put(after, after, up_two.T, one_eye)


def factor(row, block, columns):
    lead = block.shape[1]
    rows = columns.shape[0]
    fixed = lambda *shape: pl.BlockSpec(shape, lambda i: (0, 0))
    return pl.pallas_call(
        factor_kernel,
        grid=(1,),
        out_shape=(
            jax.ShapeDtypeStruct((rows, lead), f32),
            jax.ShapeDtypeStruct((rows, lead), bf16),
            jax.ShapeDtypeStruct((rows, lead), bf16),
        ),
        in_specs=[pl.BlockSpec(memory_space=pltpu.SMEM), fixed(lead, lead), fixed(rows, lead)],
        out_specs=(fixed(rows, lead),) * 3,
        compiler_params=pltpu.CompilerParams(vmem_limit_bytes=VMEM_LIMIT),
        name="factor",
    )(row, block, columns)


def local_fast(frontal, child_tiles, child_rows, child_cols):
    rows, order = frontal.shape
    side = child_tiles.shape[1]
    lead = 2 * side
    tile_rows = order // side
    devices = lax.axis_size("row")
    layers = devices // 4
    slots = MOST_SAME * rows // side
    row = lax.axis_index("row").astype(jnp.int32)
    every = [(z, x, c) for z in range(layers) for x in range(2) for c in range(2)]
    index = lambda z, x, c: z % layers * 4 + x * 2 + c
    over_core = [(index(z, x, c), index(z, x, 1 - c)) for z, x, c in every]
    over_x = [(index(z, x, c), index(z, 1 - x, c)) for z, x, c in every]
    over_z = lambda s: [(index(z, x, c), index(z + s, x, c)) for z, x, c in every]
    send = lambda x, pairs: lax.ppermute(x, "row", pairs)
    exchange = lambda x: lax.all_to_all(x, "row", split_axis=0, concat_axis=0, tiled=True)

    first, second, third = pack(child_tiles, child_rows, child_cols, devices, tile_rows)
    one = exchange(first)
    head = one[:, FIRST * side : FIRST * side + 2, :slots].astype(f32)
    labels = head[:, 0].astype(jnp.int32) - 1
    flags = jnp.max(head[:, 1, :2], axis=0)
    flags = jnp.maximum(flags, lax.ppermute(flags, "groups", [(0, 1), (1, 0)]))

    def late_lead(second, third, labels):
        rest = jnp.concatenate([exchange(second), exchange(third)], axis=1)
        rest = rest.reshape(devices * (slots - FIRST), side, side)
        late = labels[:, FIRST:].reshape(-1)
        keep = late[:, None] == (jnp.arange(rows // side)[:, None] * tile_rows + jnp.arange(2)[None, :]).reshape(1, -1)
        total = jnp.einsum("nk,nab->kab", keep.astype(bf16), rest, preferred_element_type=f32)
        return total.reshape(rows // side, 2, side, side).transpose(0, 2, 1, 3).reshape(rows, lead)

    more = lax.cond(
        flags[0] > 0, late_lead, lambda *_: jnp.zeros((rows, lead), f32), second, third, labels
    )
    columns = lead_columns(labels, frontal[:, :lead], more, one, tile_rows)

    row_ids, col_ids = jnp.arange(rows)[:, None], jnp.arange(lead)[None, :]
    diagonal = jnp.sum(jnp.where(row_ids == col_ids, columns, 0.0), axis=0)
    lost = (diagonal - lax.reduce_precision(diagonal, 5, 10)).reshape(2, side)
    lost = jnp.pad(lost, ((0, rows - 2), (side, 0)))
    narrow = jnp.where((row == 0) & (row_ids < 2) & (col_ids >= side), lost, columns).astype(f16)
    narrow, second = lax.optimization_barrier((narrow, second))

    lane = [narrow] + [send(narrow, over_z(s)) for s in range(1, layers)]
    early = jnp.concatenate([lane[0], lane[1]], axis=0)
    late = jnp.concatenate(lane[2:], axis=0)
    parts = []
    for part in (early, late):
        both = jnp.concatenate([part, send(part, over_x)], axis=0)
        parts += [both, send(both, over_core)]
    parts[-1], second = lax.optimization_barrier((parts[-1], second))
    two = exchange(second)
    wide = jnp.concatenate(parts, axis=0).astype(f32)
    hi = lax.reduce_precision(wide, 8, 7)
    lo = (wide - hi).astype(bf16)
    hi = hi.astype(bf16)
    ids = jnp.arange(devices, dtype=jnp.int32)
    shift, dx, dc = (row // 4 - ids // 4) % layers, (ids // 2 % 2) ^ (row // 2 % 2), (ids % 2) ^ (row % 2)
    place_of = jnp.where(
        shift < 2, dc * 4 + dx * 2 + shift, 8 + dc * 2 * (layers - 2) + dx * (layers - 2) + shift - 2
    )
    start = place_of[0] * rows
    block = lax.dynamic_slice(hi, (start, 0), (lead, lead)).astype(f32) + lax.dynamic_slice(
        lo, (start, 0), (lead, lead)
    ).astype(f32)

    panel, whi, wlo = factor(row[None], block, columns)
    front = update(frontal, panel, whi, wlo, hi, lo, place_of)

    wanted = jnp.where(labels % tile_rows < 2, -1, labels)
    front = place(front, wanted[:, :FIRST], one, tile_rows)
    front, two = lax.optimization_barrier((front, two))
    front = place(front, wanted[:, FIRST : FIRST + SECOND], two, tile_rows)
    front, third, labels = lax.optimization_barrier((front, third, wanted[:, FIRST + SECOND :]))
    return lax.cond(
        flags[1] > 0,
        lambda front, third, labels: place(front, labels, exchange(third), tile_rows),
        lambda front, third, labels: front,
        front, third, labels,
    )


def factor_rows(column_block, square_block, low_edge):
    tile_side = square_block.shape[0]
    factor = jnp.linalg.cholesky(square_block)
    identity = jnp.eye(tile_side, dtype=column_block.dtype)
    inverse = jax.scipy.linalg.solve_triangular(factor, identity, lower=True)
    solved = jnp.dot(column_block, inverse.T, precision=highest)
    row_ids = jnp.arange(column_block.shape[0], dtype=jnp.int32)
    inside = (row_ids >= low_edge) & (row_ids < low_edge + tile_side)
    within = jnp.take(factor, jnp.clip(row_ids - low_edge, 0, tile_side - 1), axis=0)
    before = row_ids < low_edge
    return jnp.where(
        inside[:, None], within, jnp.where(before[:, None], jnp.zeros_like(solved), solved)
    )


def apply_panel(current, panel_rows, update, low_edge):
    tile_side = panel_rows.shape[1]
    col_ids = jnp.arange(current.shape[1], dtype=jnp.int32)[None, :]
    current = jnp.where(col_ids >= low_edge + tile_side, current - update, current)
    return current.at[:, low_edge : low_edge + tile_side].set(panel_rows)


def pack_pieces(child_tiles, child_rows, child_cols, selected, rows_dev, order):
    tile_total = child_tiles.shape[0]
    tile_side = child_tiles.shape[1]
    tile_rows = order // tile_side
    piece_rows = min(rows_dev, tile_side)
    per_tile = tile_side // piece_rows
    capacity = MOST_SAME * max(1, rows_dev // tile_side)
    devices = lax.axis_size("row")
    parent = child_rows[:, 0]
    grouping = parent * tile_side // max(rows_dev, tile_side)
    sequence = jnp.arange(tile_total, dtype=jnp.int32)
    earlier = (
        (grouping[:, None] == grouping[None, :])
        & (sequence[None, :] < sequence[:, None])
        & selected[None, :]
    )
    slot_ids = jnp.sum(earlier.astype(jnp.int32), axis=1)
    offsets = (
        parent[:, None] * tile_side + jnp.arange(per_tile, dtype=jnp.int32)[None, :] * piece_rows
    )
    targets = jnp.where(selected[:, None], offsets // rows_dev, devices)
    local_ids = offsets % rows_dev // piece_rows
    slot_grid = jnp.broadcast_to(slot_ids[:, None], targets.shape)
    pieces = child_tiles.reshape(tile_total, per_tile, piece_rows, tile_side)
    outgoing = (
        jnp.zeros((devices, capacity, piece_rows, tile_side), child_tiles.dtype)
        .at[targets, slot_grid]
        .set(pieces, mode="drop")
    )
    position = local_ids * tile_rows + child_cols[:, None]
    labels = (
        jnp.full((devices, capacity), -1, jnp.int32)
        .at[targets, slot_grid]
        .set(position, mode="drop")
    )
    return (outgoing, labels)


def place_pieces(arrived, arrived_ids, rows_dev, order):
    piece_rows = arrived.shape[2]
    tile_side = arrived.shape[3]
    tile_rows = order // tile_side
    blocks_dev = rows_dev // piece_rows
    count = arrived.shape[0] * arrived.shape[1]
    selector = (
        arrived_ids.reshape(-1, 1) == jnp.arange(blocks_dev * tile_rows, dtype=jnp.int32)[None, :]
    ).astype(arrived.dtype)
    selector = selector.reshape(count, blocks_dev, tile_rows)
    flattened = arrived.reshape(count, piece_rows, tile_side)
    assembled_part = jnp.einsum(
        "nqc,nsw->qscw", selector, flattened, preferred_element_type=jnp.float32
    )
    return assembled_part.reshape(rows_dev, order)


def local_small(frontal, child_tiles, child_rows, child_cols):
    rows_dev = frontal.shape[0]
    order = frontal.shape[1]
    tile_side = child_tiles.shape[1]
    first_row = lax.axis_index("row") * rows_dev
    current = frontal
    everything = jnp.ones(child_cols.shape, dtype=bool)
    outgoing, labels = pack_pieces(child_tiles, child_rows, child_cols, everything, rows_dev, order)
    arrived, arrived_ids = (
        lax.all_to_all(outgoing, "row", split_axis=0, concat_axis=0, tiled=True),
        lax.all_to_all(labels, "row", split_axis=0, concat_axis=0, tiled=True),
    )
    current = current + place_pieces(arrived, arrived_ids, rows_dev, order)
    leading = lax.all_gather(current[:, : 2 * tile_side], "row", axis=0, tiled=True)
    first_all = factor_rows(leading[:, :tile_side], leading[:tile_side, :tile_side], 0)
    second_block = leading[:, tile_side:] - jnp.dot(
        first_all, first_all[tile_side : 2 * tile_side].T, precision=highest
    )
    second_all = factor_rows(second_block, second_block[tile_side : 2 * tile_side], tile_side)
    for panel_index, panel_all in enumerate((first_all, second_all)):
        low_edge = panel_index * tile_side
        panel_own = lax.dynamic_slice_in_dim(panel_all, first_row, rows_dev, 0)
        update = jnp.dot(panel_own, panel_all.T, precision=highest)
        current = apply_panel(current, panel_own, update, low_edge)
    return current


def local(frontal, child_tiles, child_rows, child_cols):
    rows, order = frontal.shape
    side = child_tiles.shape[1]
    devices = lax.axis_size("row")
    wide = rows >= 2 * side and rows % side == 0 and MOST_SAME * rows // side > FIRST + SECOND
    if wide and order == devices * rows and devices % 4 == 0 and lax.axis_size("groups") == 2:
        return local_fast(frontal, child_tiles, child_rows, child_cols)
    return local_small(frontal, child_tiles, child_rows, child_cols)


def solution(mesh):
    return jax.shard_map(
        local,
        mesh=mesh,
        in_specs=(
            P(("groups", "row"), None),
            P(("groups", "row"), None, None),
            P(("groups", "row"), None),
            P(("groups", "row")),
        ),
        out_specs=P(("groups", "row"), None),
        check_vma=False,
    )
```

```python
import functools
import jax
import jax.numpy as jnp
from jax import lax
from jax.experimental import pallas as pl
from jax.experimental.pallas import tpu as pltpu
from jax.sharding import PartitionSpec as P

MOST_SAME = 2
FIRST = 3
SECOND = 3
HEAD = 16
VMEM_LIMIT = 56 << 20


highest = lax.Precision.HIGHEST
f32, bf16 = jnp.float32, jnp.bfloat16


def loop(count, body):
    lax.fori_loop(0, count, lambda i, carry: (body(i), carry)[1], 0)


def pack_kernel(
    tile_rows, per_dev, rows_ref, cols_ref, tiles_ref, first_ref, second_ref, third_ref,
    heads, heads_out, counts, sems, head_sem,
):
    tiles, side, _ = tiles_ref.shape
    devices = first_ref.shape[0]
    lanes = lax.broadcasted_iota(jnp.int32, (8, 128), 1)
    subs = lax.broadcasted_iota(jnp.int32, (8, 128), 0)
    heads[...] = jnp.zeros_like(heads)

    def clear(d):
        counts[d] = 0

    loop(devices, clear)

    def place(i, wanted):
        row, col = rows_ref[i], cols_ref[i]

        @pl.when((col < 2) == wanted)
        def _():
            d, q = row // per_dev, row % per_dev
            s = counts[d]
            counts[d] = s + 1
            here = (lanes == s) & (subs == 0)
            heads[d] = jnp.where(here, (q * tile_rows + col + 1).astype(f32), heads[d])

            @pl.when(s < FIRST)
            def _():
                pltpu.make_async_copy(
                    tiles_ref.at[i], first_ref.at[d, pl.ds(s * side, side)], sems.at[i]
                ).start()

            @pl.when((s >= FIRST) & (s < FIRST + SECOND))
            def _():
                pltpu.make_async_copy(
                    tiles_ref.at[i], second_ref.at[d, pl.ds((s - FIRST) * side, side)], sems.at[i]
                ).start()

            @pl.when(s >= FIRST + SECOND)
            def _():
                pltpu.make_async_copy(
                    tiles_ref.at[i],
                    third_ref.at[d, pl.ds((s - FIRST - SECOND) * side, side)],
                    sems.at[i],
                ).start()

    def most():
        return lax.fori_loop(0, devices, lambda d, m: jnp.maximum(m, counts[d]), 0)

    loop(tiles, lambda i: place(i, True))
    lead_over = (most() > FIRST).astype(f32)
    loop(tiles, lambda i: place(i, False))
    over = (most() > FIRST + SECOND).astype(f32)
    flags = jnp.where(lanes == 0, lead_over, jnp.where(lanes == 1, over, 0.0))
    marked = jnp.where((subs == 1)[None], flags[None], heads[...])
    heads_out[...] = jnp.concatenate([marked, jnp.zeros_like(marked)], axis=1).astype(bf16)
    copy = pltpu.make_async_copy(heads_out, first_ref.at[:, pl.ds(FIRST * side, HEAD)], head_sem)
    copy.start()

    def finish(i):
        pltpu.make_async_copy(tiles_ref.at[i], first_ref.at[0, pl.ds(0, side)], sems.at[i]).wait()

    loop(tiles, finish)
    copy.wait()


def pack(child_tiles, child_rows, child_cols, devices, tile_rows):
    tiles, side, _ = child_tiles.shape
    per_dev = tile_rows // devices
    third = MOST_SAME * per_dev - FIRST - SECOND
    smem, anyw = (pl.BlockSpec(memory_space=m) for m in (pltpu.SMEM, pl.ANY))
    return pl.pallas_call(
        functools.partial(pack_kernel, tile_rows, per_dev),
        grid=(1,),
        out_shape=(
            jax.ShapeDtypeStruct((devices, FIRST * side + HEAD, side), bf16),
            jax.ShapeDtypeStruct((devices, SECOND * side, side), bf16),
            jax.ShapeDtypeStruct((devices, third * side, side), bf16),
        ),
        in_specs=[smem, smem, pl.BlockSpec((tiles, side, side), lambda i: (0, 0, 0))],
        out_specs=(anyw, anyw, anyw),
        scratch_shapes=[
            pltpu.VMEM((devices, 8, 128), f32),
            pltpu.VMEM((devices, HEAD, 128), bf16),
            pltpu.SMEM((devices,), jnp.int32),
            pltpu.SemaphoreType.DMA((tiles,)),
            pltpu.SemaphoreType.DMA,
        ],
        compiler_params=pltpu.CompilerParams(vmem_limit_bytes=VMEM_LIMIT),
        name="pack",
    )(child_rows[:, 0], child_cols, child_tiles)


def lead_kernel(tile_rows, slots, row_ref, labels_ref, front_ref, tiles_ref, out_ref, coded_ref):
    side = tiles_ref.shape[2]
    rows, lead = out_ref.shape
    out_ref[...] = front_ref[...]

    def body(n):
        d, s = n // FIRST, n % FIRST
        label = labels_ref[d * slots + s]
        q, col = label // tile_rows, label % tile_rows

        @pl.when((label >= 0) & (col < 2))
        def _():
            at = (pl.ds(pl.multiple_of(q * side, side), side),
                  pl.ds(pl.multiple_of(col * side, side), side))
            out_ref[at] = out_ref[at] + tiles_ref[d, pl.ds(pl.multiple_of(s * side, side), side)].astype(f32)

    loop(tiles_ref.shape[0] * FIRST, body)
    low, high = -32768.0, 32767.0
    turned = out_ref[...].T
    on = lax.broadcasted_iota(jnp.int32, turned.shape, 0) == lax.broadcasted_iota(jnp.int32, turned.shape, 1)
    diagonal = jnp.sum(jnp.where(on, turned, 0.0), axis=0, keepdims=True)
    turned = jnp.where(on & (row_ref[0] == 0), 0.0, turned)

    def power(most):
        return jnp.ceil(jnp.log2(jnp.maximum(most, 1e-30))) - 15.0

    scale = power(jnp.max(jnp.abs(turned), axis=0, keepdims=True))
    values = jnp.clip(jnp.round(turned * jnp.exp2(-scale)), low, high)
    coded_ref[0, :lead] = values.astype(jnp.int32).astype(jnp.int16)
    own = power(jnp.abs(diagonal))
    wide = diagonal * jnp.exp2(-own)
    upper = jnp.clip(jnp.round(wide), low, high)
    lower = jnp.clip(jnp.round((wide - upper) * 32768.0), low, high)
    subs = lax.broadcasted_iota(jnp.int32, (HEAD, rows), 0)
    head = jnp.zeros((HEAD, rows), f32)
    for i, value in enumerate((scale, own, upper, lower)):
        head = jnp.where(subs == i, value, head)
    coded_ref[0, lead:] = head.astype(jnp.int32).astype(jnp.int16)


def lead_columns(row, labels, frontal, arrived, tile_rows):
    rows = frontal.shape[0]
    lead = 2 * arrived.shape[2]
    smem = pl.BlockSpec(memory_space=pltpu.SMEM)
    return pl.pallas_call(
        functools.partial(lead_kernel, tile_rows, labels.shape[1]),
        grid=(1,),
        out_shape=(
            jax.ShapeDtypeStruct((rows, lead), f32),
            jax.ShapeDtypeStruct((1, lead + HEAD, rows), jnp.int16),
        ),
        in_specs=[
            smem, smem,
            pl.BlockSpec((rows, lead), lambda i: (0, 0)),
            pl.BlockSpec(arrived.shape, lambda i: (0, 0, 0)),
        ],
        out_specs=(
            pl.BlockSpec((rows, lead), lambda i: (0, 0)),
            pl.BlockSpec((1, lead + HEAD, rows), lambda i: (0, 0, 0)),
        ),
        compiler_params=pltpu.CompilerParams(vmem_limit_bytes=VMEM_LIMIT),
        name="lead_columns",
    )(row, labels.reshape(-1), frontal, arrived)


def place_kernel(tile_rows, labels_ref, owner_ref, tiles_ref, front_ref, out_ref, held, listed, in_sems, out_sems):
    side = tiles_ref.shape[2]
    slots = tiles_ref.shape[1] // side

    def spot(n):
        label = labels_ref[n]
        q, col = label // tile_rows, label % tile_rows
        return out_ref.at[pl.ds(pl.multiple_of(q * side, side), side), pl.ds(pl.multiple_of(col * side, side), side)]

    def fetch(n, used):
        listed[used] = n

        @pl.when(owner_ref[n] == n)
        def _():
            pltpu.make_async_copy(spot(n), held.at[n], in_sems.at[n]).start()

        return used + (labels_ref[n] >= 0).astype(jnp.int32)

    def add(i):
        n = listed[i]
        m = owner_ref[n]

        @pl.when(m == n)
        def _():
            pltpu.make_async_copy(spot(n), held.at[n], in_sems.at[n]).wait()

        held[m] += tiles_ref[n // slots, pl.ds(pl.multiple_of(n % slots * side, side), side)].astype(f32)

    def put(i):
        n = listed[i]

        @pl.when(owner_ref[n] == n)
        def _():
            pltpu.make_async_copy(held.at[n], spot(n), out_sems.at[n]).start()

    def finish(i):
        n = listed[i]

        @pl.when(owner_ref[n] == n)
        def _():
            pltpu.make_async_copy(held.at[n], spot(n), out_sems.at[n]).wait()

    used = lax.fori_loop(0, tiles_ref.shape[0] * slots, fetch, 0)
    for step in (add, put, finish):
        loop(used, step)


def place(front, labels, tiles, tile_rows):
    side = tiles.shape[2]
    labels = labels.reshape(-1)
    size = labels.size
    ids = jnp.arange(size, dtype=jnp.int32)
    owner = jnp.min(jnp.where(labels[:, None] == labels[None, :], ids[None, :], size), axis=1)
    owner = jnp.where(labels < 0, -1, owner)
    smem = pl.BlockSpec(memory_space=pltpu.SMEM)
    return pl.pallas_call(
        functools.partial(place_kernel, tile_rows),
        grid=(1,),
        out_shape=jax.ShapeDtypeStruct(front.shape, f32),
        in_specs=[smem, smem, pl.BlockSpec(tiles.shape, lambda i: (0, 0, 0)), pl.BlockSpec(memory_space=pl.ANY)],
        out_specs=pl.BlockSpec(memory_space=pl.ANY),
        input_output_aliases={3: 0},
        scratch_shapes=[
            pltpu.VMEM((size, side, side), f32),
            pltpu.SMEM((size + 1,), jnp.int32),
            pltpu.SemaphoreType.DMA((size,)),
            pltpu.SemaphoreType.DMA((size,)),
        ],
        compiler_params=pltpu.CompilerParams(vmem_limit_bytes=VMEM_LIMIT),
        name="place",
    )(labels, owner, tiles, front)


def bdot(a, b, dims):
    return lax.dot_general(a, b, (dims, ((), ())), precision=highest, preferred_element_type=f32)


STEP = 4


def eliminate(block):
    side = block.shape[0]
    lanes = lax.broadcasted_iota(jnp.int32, (1, side), 1)
    left = block
    right = jnp.where(
        lax.broadcasted_iota(jnp.int32, (side, side), 0) == lax.broadcasted_iota(jnp.int32, (side, side), 1), 1.0, 0.0
    )
    upper_rows, inverse_rows = [], []
    for k in range(0, side, STEP):
        base = k // 8 * 8
        cut = base - (side - left.shape[0])
        left, right = left[cut:], right[cut:]
        height = left.shape[0]
        wide = [jnp.broadcast_to(left[:, k + i : k + i + 1], (height, side)) for i in range(STEP)]
        cols, ups, invs = [], [], []
        for i in range(STEP):
            at = k + i - base
            col, up, inv = wide[i], left[at : at + 1], right[at : at + 1]
            for j in range(i):
                factor = cols[j][at : at + 1]
                col = col - cols[j] * factor
                up = up - ups[j] * factor
                inv = inv - invs[j] * factor
            scale = lax.rsqrt(col[at : at + 1])
            cols.append(col * scale)
            ups.append(up * scale)
            invs.append(inv * scale)
            upper_rows.append(jnp.where(lanes >= k + i, ups[i], 0.0))
            inverse_rows.append(invs[i])
        for i in range(STEP):
            left = left - cols[i] * ups[i]
            right = right - cols[i] * invs[i]
    return jnp.concatenate(upper_rows, axis=0), jnp.concatenate(inverse_rows, axis=0)


def decode_block(coded, lead):
    head = coded[lead:].astype(jnp.int32).astype(f32)[:, :lead]
    block = coded[:lead, :lead].astype(jnp.int32).astype(f32) * jnp.exp2(head[0:1])
    diagonal = (head[2:3] + head[3:4] * (1.0 / 32768.0)) * jnp.exp2(head[1:2])
    on = lax.broadcasted_iota(jnp.int32, block.shape, 0) == lax.broadcasted_iota(jnp.int32, block.shape, 1)
    return jnp.where(on, diagonal, block)


def factor(first, block, columns_ref, panel_ref, weights_ref):
    rows, lead = columns_ref.shape
    side = lead // 2
    eye = lax.broadcasted_iota(jnp.int32, (side, side), 0) == lax.broadcasted_iota(jnp.int32, (side, side), 1)
    b11, b21t, b22 = block[:side, :side], block[:side, side:], block[side:, side:]
    nt, nn = ((1,), (1,)), ((1,), (0,))
    up_one, inv_one = eliminate((b11 + b11.T) * 0.5)
    below = bdot(b21t.T, inv_one, nt)
    up_two, inv_two = eliminate((b22 + b22.T) * 0.5 - bdot(below, below, nt))
    corner = -bdot(inv_two, bdot(below, inv_one, nn), nn)
    left, right = columns_ref[:, :side], columns_ref[:, side:]
    panel_left = bdot(left, inv_one, nt)
    panel_right = bdot(left, corner, nt) + bdot(right, inv_two, nt)
    weight_left = bdot(panel_left, inv_one, nn) + bdot(panel_right, corner, nn)
    weight_right = bdot(panel_right, inv_two, nn)

    def put(low, cols, panel, weight):
        high = low + panel.shape[0]
        panel_ref[low:high, cols] = panel
        hi = weight.astype(bf16)
        weights_ref[low:high, cols] = hi
        weights_ref[rows + low : rows + high, cols] = (weight - hi.astype(f32)).astype(bf16)

    before, after = slice(0, side), slice(side, lead)
    put(0, before, panel_left, weight_left)
    put(0, after, panel_right, weight_right)

    @pl.when(first == 0)
    def _():
        one_eye, zero = jnp.where(eye, 1.0, 0.0), jnp.zeros((side, side), f32)
        put(0, before, up_one.T, one_eye)
        put(0, after, zero, zero)
        put(side, before, below, zero)
        put(side, after, up_two.T, one_eye)


def front_kernel(tile_rows, slots, starts, info_ref, labels_ref, columns_ref, tiles_ref, front_ref, *refs):
    count = len(starts) - 1
    parts, out_ref = refs[:count], refs[count]
    held, coded, weights, panel, in_sems, part_sems, out_sems = refs[count + 1 :]
    rows, lead = columns_ref.shape
    side = tiles_ref.shape[2]
    steps = starts[-1]
    part_copies = [
        pltpu.make_async_copy(part, coded.at[pl.ds(low, high - low)], part_sems.at[i])
        for i, (part, low, high) in enumerate(zip(parts, starts, starts[1:]))
    ]
    columns_of = lambda g: pl.ds(pl.multiple_of(g * rows, rows), rows)
    in_copies = [
        pltpu.make_async_copy(front_ref.at[:, columns_of(g)], held.at[:, columns_of(g)], in_sems.at[g])
        for g in range(steps)
    ]
    for copy in part_copies + in_copies:
        copy.start()
    for copy in part_copies:
        copy.wait()
    factor(info_ref[0], decode_block(coded[info_ref[1]], lead), columns_ref, panel, weights)
    for copy in in_copies:
        copy.wait()

    def add(n):
        d, s = n // FIRST, n % FIRST
        label = labels_ref[d * slots + s]
        q, col = label // tile_rows, label % tile_rows

        @pl.when((label >= 0) & (col >= 2))
        def _():
            at = (pl.ds(pl.multiple_of(q * side, side), side),
                  pl.ds(pl.multiple_of(col * side, side), side))
            held[at] = held[at] + tiles_ref[d, pl.ds(pl.multiple_of(s * side, side), side)].astype(f32)

    loop(tiles_ref.shape[0] * FIRST, add)
    dot = functools.partial(jnp.dot, preferred_element_type=f32)

    def out_copy(g):
        at = columns_of(info_ref[2 + g])
        return pltpu.make_async_copy(held.at[:, at], out_ref.at[:, at], out_sems.at[g])

    def step(g):
        block = info_ref[2 + g]
        values = coded[g, :lead].astype(jnp.int32)
        scale = jnp.exp2(coded[g, lead:].astype(jnp.int32).astype(f32)[0:1])
        lower = ((values + 128) & 255) - 128
        hi = (values - lower).astype(f32).astype(bf16)
        lo = lower.astype(f32).astype(bf16)
        both = dot(weights[...], hi)
        total = both[:rows] + both[rows:] + dot(weights[:rows], lo)
        held[:, columns_of(block)] = held[:, columns_of(block)] - total * scale

        @pl.when(block == 0)
        def _():
            held[:, :lead] = panel[...]

        out_copy(g).start()

    loop(steps, step)
    loop(steps, lambda g: out_copy(g).wait())


def make_front(info, labels, columns, arrived, frontal, parts, tile_rows):
    rows, order = frontal.shape
    lead = columns.shape[1]
    starts = [0]
    for part in parts:
        starts.append(starts[-1] + part.shape[0])
    smem, anyw = (pl.BlockSpec(memory_space=m) for m in (pltpu.SMEM, pl.ANY))
    return pl.pallas_call(
        functools.partial(front_kernel, tile_rows, labels.shape[1], tuple(starts)),
        grid=(1,),
        out_shape=jax.ShapeDtypeStruct((rows, order), f32),
        in_specs=[
            smem, smem,
            pl.BlockSpec((rows, lead), lambda i: (0, 0)),
            pl.BlockSpec(arrived.shape, lambda i: (0, 0, 0)),
            anyw,
        ] + [anyw] * len(parts),
        out_specs=anyw,
        scratch_shapes=[
            pltpu.VMEM((rows, order), f32),
            pltpu.VMEM((starts[-1], lead + HEAD, rows), jnp.int16),
            pltpu.VMEM((2 * rows, lead), bf16),
            pltpu.VMEM((rows, lead), f32),
            pltpu.SemaphoreType.DMA((starts[-1],)),
            pltpu.SemaphoreType.DMA((len(parts),)),
            pltpu.SemaphoreType.DMA((starts[-1],)),
        ],
        compiler_params=pltpu.CompilerParams(vmem_limit_bytes=VMEM_LIMIT),
        cost_estimate=pl.CostEstimate(
            flops=6 * rows * order * lead, bytes_accessed=8 * rows * order, transcendentals=0
        ),
        name="front",
    )(info, labels.reshape(-1), columns, arrived, frontal, *parts)


def local_fast(frontal, child_tiles, child_rows, child_cols):
    rows, order = frontal.shape
    side = child_tiles.shape[1]
    lead = 2 * side
    tile_rows = order // side
    devices = lax.axis_size("row")
    layers = devices // 4
    slots = MOST_SAME * rows // side
    row = lax.axis_index("row").astype(jnp.int32)
    every = [(z, x, c) for z in range(layers) for x in range(2) for c in range(2)]
    index = lambda z, x, c: z % layers * 4 + x * 2 + c
    over_core = [(index(z, x, c), index(z, x, 1 - c)) for z, x, c in every]
    over_x = [(index(z, x, c), index(z, 1 - x, c)) for z, x, c in every]
    over_z = lambda s: [(index(z, x, c), index(z + s, x, c)) for z, x, c in every]
    send = lambda x, pairs: lax.ppermute(x, "row", pairs)
    exchange = lambda x: lax.all_to_all(x, "row", split_axis=0, concat_axis=0, tiled=True)

    first, second, third = pack(child_tiles, child_rows, child_cols, devices, tile_rows)
    one = exchange(first)
    head = one[:, FIRST * side : FIRST * side + 2, :slots].astype(f32)
    labels = head[:, 0].astype(jnp.int32) - 1
    columns, narrow = lead_columns(row[None], labels, frontal, one, tile_rows)

    join = lambda *x: jnp.concatenate(x, axis=0)
    tie = lax.optimization_barrier
    narrow, second = tie((narrow, second))
    up, down, over = send(narrow, over_z(1)), send(narrow, over_z(layers - 1)), send(narrow, over_x)
    narrow, up, down, over = tie((narrow, up, down, over))
    near, beside = join(narrow, over), join(up, down)
    far = [send(narrow, over_z(s)) for s in range(2, layers - 1)]
    beside_x, near_c = send(beside, over_x), send(near, over_core)
    far, beside_x, near_c, near, beside = tie((far, beside_x, near_c, near, beside))
    far, beside = join(*far), join(beside, beside_x)
    far_x, beside_c = send(far, over_x), send(beside, over_core)
    far_x, beside_c, far = tie((far_x, beside_c, far))
    far = join(far, far_x)
    far_c = send(far, over_core)
    far_c, second = tie((far_c, second))
    two = exchange(second)
    parts = [near, near_c, beside, beside_c, far, far_c]

    z, x, c = row // 4, row // 2 % 2, row % 2
    cols = []
    for offsets in ([0], [1, layers - 1], list(range(2, layers - 1))):
        cols += [
            (z - dz) % layers * 4 + (x ^ dx) * 2 + (c ^ dc) for dc in range(2) for dx in range(2) for dz in offsets
        ]
    at = sum(jnp.where(col == 0, g, 0) for g, col in enumerate(cols))
    info = jnp.stack([row, at] + cols).astype(jnp.int32)
    front = make_front(info, labels, columns, one, frontal, parts, tile_rows)

    wanted = jnp.where(labels % tile_rows < 2, -1, labels)
    front, two = tie((front, two))
    front = place(front, wanted[:, FIRST : FIRST + SECOND], two, tile_rows)
    flags = jnp.max(head[:, 1, :2], axis=0)
    flags = jnp.maximum(flags, lax.ppermute(flags, "groups", [(0, 1), (1, 0)]))
    front, third, labels = tie((front, third, wanted[:, FIRST + SECOND :]))
    case = jnp.where(flags[0] > 0, 2, jnp.where(flags[1] > 0, 1, 0)).astype(jnp.int32)

    def spread(x, axis):
        every = exchange(jnp.broadcast_to(x[None], (devices,) + x.shape))
        return every.reshape(order, x.shape[1])

    return lax.switch(
        case,
        [
            lambda front, third, labels, *args: front,
            lambda front, third, labels, *args: place(front, labels, exchange(third), tile_rows),
            lambda front, third, labels, *args: local_small(*args, spread),
        ],
        front, third, labels, frontal, child_tiles, child_rows, child_cols,
    )


def gather_rows(x, axis):
    return lax.all_gather(x, axis, axis=0, tiled=True)


def factor_rows(column_block, square_block, low_edge):
    tile_side = square_block.shape[0]
    factor = jnp.linalg.cholesky(square_block)
    identity = jnp.eye(tile_side, dtype=column_block.dtype)
    inverse = jax.scipy.linalg.solve_triangular(factor, identity, lower=True)
    solved = jnp.dot(column_block, inverse.T, precision=highest)
    row_ids = jnp.arange(column_block.shape[0], dtype=jnp.int32)
    inside = (row_ids >= low_edge) & (row_ids < low_edge + tile_side)
    within = jnp.take(factor, jnp.clip(row_ids - low_edge, 0, tile_side - 1), axis=0)
    before = row_ids < low_edge
    return jnp.where(
        inside[:, None], within, jnp.where(before[:, None], jnp.zeros_like(solved), solved)
    )


def apply_panel(current, panel_rows, update, low_edge):
    tile_side = panel_rows.shape[1]
    col_ids = jnp.arange(current.shape[1], dtype=jnp.int32)[None, :]
    current = jnp.where(col_ids >= low_edge + tile_side, current - update, current)
    return current.at[:, low_edge : low_edge + tile_side].set(panel_rows)


def pack_pieces(child_tiles, child_rows, child_cols, selected, rows_dev, order):
    tile_total = child_tiles.shape[0]
    tile_side = child_tiles.shape[1]
    tile_rows = order // tile_side
    piece_rows = min(rows_dev, tile_side)
    per_tile = tile_side // piece_rows
    capacity = MOST_SAME * max(1, rows_dev // tile_side)
    devices = lax.axis_size("row")
    parent = child_rows[:, 0]
    grouping = parent * tile_side // max(rows_dev, tile_side)
    sequence = jnp.arange(tile_total, dtype=jnp.int32)
    earlier = (
        (grouping[:, None] == grouping[None, :])
        & (sequence[None, :] < sequence[:, None])
        & selected[None, :]
    )
    slot_ids = jnp.sum(earlier.astype(jnp.int32), axis=1)
    offsets = (
        parent[:, None] * tile_side + jnp.arange(per_tile, dtype=jnp.int32)[None, :] * piece_rows
    )
    targets = jnp.where(selected[:, None], offsets // rows_dev, devices)
    local_ids = offsets % rows_dev // piece_rows
    slot_grid = jnp.broadcast_to(slot_ids[:, None], targets.shape)
    pieces = child_tiles.reshape(tile_total, per_tile, piece_rows, tile_side)
    outgoing = (
        jnp.zeros((devices, capacity, piece_rows, tile_side), child_tiles.dtype)
        .at[targets, slot_grid]
        .set(pieces, mode="drop")
    )
    position = local_ids * tile_rows + child_cols[:, None]
    labels = (
        jnp.full((devices, capacity), -1, jnp.int32)
        .at[targets, slot_grid]
        .set(position, mode="drop")
    )
    return (outgoing, labels)


def place_pieces(arrived, arrived_ids, rows_dev, order):
    piece_rows = arrived.shape[2]
    tile_side = arrived.shape[3]
    tile_rows = order // tile_side
    blocks_dev = rows_dev // piece_rows
    count = arrived.shape[0] * arrived.shape[1]
    selector = (
        arrived_ids.reshape(-1, 1) == jnp.arange(blocks_dev * tile_rows, dtype=jnp.int32)[None, :]
    ).astype(arrived.dtype)
    selector = selector.reshape(count, blocks_dev, tile_rows)
    flattened = arrived.reshape(count, piece_rows, tile_side)
    assembled_part = jnp.einsum(
        "nqc,nsw->qscw", selector, flattened, preferred_element_type=jnp.float32
    )
    return assembled_part.reshape(rows_dev, order)


def local_small(frontal, child_tiles, child_rows, child_cols, gather):
    rows_dev = frontal.shape[0]
    order = frontal.shape[1]
    tile_side = child_tiles.shape[1]
    first_row = lax.axis_index("row") * rows_dev
    current = frontal
    everything = jnp.ones(child_cols.shape, dtype=bool)
    outgoing, labels = pack_pieces(child_tiles, child_rows, child_cols, everything, rows_dev, order)
    arrived, arrived_ids = (
        lax.all_to_all(outgoing, "row", split_axis=0, concat_axis=0, tiled=True),
        lax.all_to_all(labels, "row", split_axis=0, concat_axis=0, tiled=True),
    )
    current = current + place_pieces(arrived, arrived_ids, rows_dev, order)
    leading = gather(current[:, : 2 * tile_side], "row")
    first_all = factor_rows(leading[:, :tile_side], leading[:tile_side, :tile_side], 0)
    second_block = leading[:, tile_side:] - jnp.dot(
        first_all, first_all[tile_side : 2 * tile_side].T, precision=highest
    )
    second_all = factor_rows(second_block, second_block[tile_side : 2 * tile_side], tile_side)
    for panel_index, panel_all in enumerate((first_all, second_all)):
        low_edge = panel_index * tile_side
        panel_own = lax.dynamic_slice_in_dim(panel_all, first_row, rows_dev, 0)
        update = jnp.dot(panel_own, panel_all.T, precision=highest)
        current = apply_panel(current, panel_own, update, low_edge)
    return current


def local(frontal, child_tiles, child_rows, child_cols):
    rows, order = frontal.shape
    side = child_tiles.shape[1]
    devices = lax.axis_size("row")
    wide = rows >= 2 * side and rows % side == 0 and MOST_SAME * rows // side > FIRST + SECOND
    if wide and order == devices * rows and devices % 4 == 0 and devices >= 16 and lax.axis_size("groups") == 2:
        return local_fast(frontal, child_tiles, child_rows, child_cols)
    return local_small(frontal, child_tiles, child_rows, child_cols, gather_rows)


def solution(mesh):
    return jax.shard_map(
        local,
        mesh=mesh,
        in_specs=(
            P(("groups", "row"), None),
            P(("groups", "row"), None, None),
            P(("groups", "row"), None),
            P(("groups", "row")),
        ),
        out_specs=P(("groups", "row"), None),
        check_vma=False,
    )
```

```python
import functools
import jax
import jax.numpy as jnp
from jax import lax
from jax.experimental import pallas as pl
from jax.experimental.pallas import tpu as pltpu
from jax.sharding import PartitionSpec as P

MOST_SAME = 2
FIRST = 3
SECOND = 3
HEAD = 16
VMEM_LIMIT = 56 << 20


highest = lax.Precision.HIGHEST
f32, bf16 = jnp.float32, jnp.bfloat16


def loop(count, body, unroll=1):
    lax.fori_loop(0, count, lambda i, carry: (body(i), carry)[1], 0, unroll=unroll)


def pack_kernel(
    tile_rows, per_dev, rows_ref, cols_ref, tiles_ref, first_ref, second_ref, third_ref,
    heads, heads_out, counts, sem, head_sem,
):
    tiles, side, _ = tiles_ref.shape
    devices = first_ref.shape[0]
    lanes = lax.broadcasted_iota(jnp.int32, (8, 128), 1)
    subs = lax.broadcasted_iota(jnp.int32, (8, 128), 0)
    heads[...] = jnp.zeros_like(heads)

    def clear(d):
        counts[d] = 0

    loop(devices, clear)

    def place(i, wanted):
        row, col = rows_ref[i], cols_ref[i]

        @pl.when((col < 2) == wanted)
        def _():
            d, q = row // per_dev, row % per_dev
            s = counts[d]
            counts[d] = s + 1
            here = (lanes == s) & (subs == 0)
            heads[d] = jnp.where(here, (q * tile_rows + col + 1).astype(f32), heads[d])

            @pl.when(s < FIRST)
            def _():
                pltpu.make_async_copy(
                    tiles_ref.at[i], first_ref.at[d, pl.ds(s * side, side)], sem
                ).start()

            @pl.when((s >= FIRST) & (s < FIRST + SECOND))
            def _():
                pltpu.make_async_copy(
                    tiles_ref.at[i], second_ref.at[d, pl.ds((s - FIRST) * side, side)], sem
                ).start()

            @pl.when(s >= FIRST + SECOND)
            def _():
                pltpu.make_async_copy(
                    tiles_ref.at[i],
                    third_ref.at[d, pl.ds((s - FIRST - SECOND) * side, side)],
                    sem,
                ).start()

    def most():
        return lax.fori_loop(0, devices, lambda d, m: jnp.maximum(m, counts[d]), 0)

    loop(tiles, lambda i: place(i, True), 4)
    lead_over = (most() > FIRST).astype(f32)
    loop(tiles, lambda i: place(i, False), 4)
    over = (most() > FIRST + SECOND).astype(f32)
    flags = jnp.where(lanes == 0, lead_over, jnp.where(lanes == 1, over, 0.0))
    marked = jnp.where((subs == 1)[None], flags[None], heads[...])
    heads_out[...] = jnp.concatenate([marked, jnp.zeros_like(marked)], axis=1).astype(bf16)
    copy = pltpu.make_async_copy(heads_out, first_ref.at[:, pl.ds(FIRST * side, HEAD)], head_sem)
    copy.start()

    pltpu.make_async_copy(tiles_ref, tiles_ref, sem).wait()
    copy.wait()


def pack(child_tiles, child_rows, child_cols, devices, tile_rows):
    tiles, side, _ = child_tiles.shape
    per_dev = tile_rows // devices
    third = MOST_SAME * per_dev - FIRST - SECOND
    smem, anyw = (pl.BlockSpec(memory_space=m) for m in (pltpu.SMEM, pl.ANY))
    return pl.pallas_call(
        functools.partial(pack_kernel, tile_rows, per_dev),
        grid=(1,),
        out_shape=(
            jax.ShapeDtypeStruct((devices, FIRST * side + HEAD, side), bf16),
            jax.ShapeDtypeStruct((devices, SECOND * side, side), bf16),
            jax.ShapeDtypeStruct((devices, third * side, side), bf16),
        ),
        in_specs=[smem, smem, pl.BlockSpec((tiles, side, side), lambda i: (0, 0, 0))],
        out_specs=(anyw, anyw, anyw),
        scratch_shapes=[
            pltpu.VMEM((devices, 8, 128), f32),
            pltpu.VMEM((devices, HEAD, 128), bf16),
            pltpu.SMEM((devices,), jnp.int32),
            pltpu.SemaphoreType.DMA,
            pltpu.SemaphoreType.DMA,
        ],
        compiler_params=pltpu.CompilerParams(vmem_limit_bytes=VMEM_LIMIT),
        name="pack",
    )(child_rows[:, 0], child_cols, child_tiles)


def lead_kernel(tile_rows, slots, row_ref, labels_ref, front_ref, tiles_ref, out_ref, coded_ref):
    side = tiles_ref.shape[2]
    rows, lead = out_ref.shape
    out_ref[...] = front_ref[...]

    def body(n):
        d, s = n // FIRST, n % FIRST
        label = labels_ref[d * slots + s]
        q, col = label // tile_rows, label % tile_rows

        @pl.when((label >= 0) & (col < 2))
        def _():
            at = (pl.ds(pl.multiple_of(q * side, side), side),
                  pl.ds(pl.multiple_of(col * side, side), side))
            out_ref[at] = out_ref[at] + tiles_ref[d, pl.ds(pl.multiple_of(s * side, side), side)].astype(f32)

    loop(tiles_ref.shape[0] * FIRST, body)
    low, high = -32768.0, 32767.0
    turned = out_ref[...].T
    on = lax.broadcasted_iota(jnp.int32, turned.shape, 0) == lax.broadcasted_iota(jnp.int32, turned.shape, 1)
    diagonal = jnp.sum(jnp.where(on, turned, 0.0), axis=0, keepdims=True)
    turned = jnp.where(on & (row_ref[0] == 0), 0.0, turned)

    def power(most):
        return jnp.ceil(jnp.log2(jnp.maximum(most, 1e-30))) - 15.0

    scale = power(jnp.max(jnp.abs(turned), axis=0, keepdims=True))
    values = jnp.clip(jnp.round(turned * jnp.exp2(-scale)), low, high)
    coded_ref[0, :lead] = values.astype(jnp.int32).astype(jnp.int16)
    own = power(jnp.abs(diagonal))
    wide = diagonal * jnp.exp2(-own)
    upper = jnp.clip(jnp.round(wide), low, high)
    lower = jnp.clip(jnp.round((wide - upper) * 32768.0), low, high)
    subs = lax.broadcasted_iota(jnp.int32, (HEAD, rows), 0)
    head = jnp.zeros((HEAD, rows), f32)
    for i, value in enumerate((scale, own, upper, lower)):
        head = jnp.where(subs == i, value, head)
    coded_ref[0, lead:] = head.astype(jnp.int32).astype(jnp.int16)


def lead_columns(row, labels, frontal, arrived, tile_rows):
    rows = frontal.shape[0]
    lead = 2 * arrived.shape[2]
    smem = pl.BlockSpec(memory_space=pltpu.SMEM)
    return pl.pallas_call(
        functools.partial(lead_kernel, tile_rows, labels.shape[1]),
        grid=(1,),
        out_shape=(
            jax.ShapeDtypeStruct((rows, lead), f32),
            jax.ShapeDtypeStruct((1, lead + HEAD, rows), jnp.int16),
        ),
        in_specs=[
            smem, smem,
            pl.BlockSpec((rows, lead), lambda i: (0, 0)),
            pl.BlockSpec(arrived.shape, lambda i: (0, 0, 0)),
        ],
        out_specs=(
            pl.BlockSpec((rows, lead), lambda i: (0, 0)),
            pl.BlockSpec((1, lead + HEAD, rows), lambda i: (0, 0, 0)),
        ),
        compiler_params=pltpu.CompilerParams(vmem_limit_bytes=VMEM_LIMIT),
        name="lead_columns",
    )(row, labels.reshape(-1), frontal, arrived)


def place_kernel(
    tile_rows, labels_ref, owner_ref, arrived_ref, front_ref, out_ref, tiles_ref, held, listed, tile_sem, in_sems, out_sems
):
    side = tiles_ref.shape[2]
    slots = tiles_ref.shape[1] // side
    tile_copy = pltpu.make_async_copy(arrived_ref, tiles_ref, tile_sem)
    tile_copy.start()

    def spot(n):
        label = labels_ref[n]
        q, col = label // tile_rows, label % tile_rows
        return out_ref.at[pl.ds(pl.multiple_of(q * side, side), side), pl.ds(pl.multiple_of(col * side, side), side)]

    def fetch(n, used):
        listed[used] = n

        @pl.when(owner_ref[n] == n)
        def _():
            pltpu.make_async_copy(spot(n), held.at[n], in_sems.at[n]).start()

        return used + (labels_ref[n] >= 0).astype(jnp.int32)

    def add(i):
        n = listed[i]
        m = owner_ref[n]

        @pl.when(m == n)
        def _():
            pltpu.make_async_copy(spot(n), held.at[n], in_sems.at[n]).wait()

        held[m] += tiles_ref[n // slots, pl.ds(pl.multiple_of(n % slots * side, side), side)].astype(f32)

    def put(i):
        n = listed[i]

        @pl.when(owner_ref[n] == n)
        def _():
            pltpu.make_async_copy(held.at[n], spot(n), out_sems.at[n]).start()

    def finish(i):
        n = listed[i]

        @pl.when(owner_ref[n] == n)
        def _():
            pltpu.make_async_copy(held.at[n], spot(n), out_sems.at[n]).wait()

    used = lax.fori_loop(0, tiles_ref.shape[0] * slots, fetch, 0, unroll=4)
    tile_copy.wait()
    for step in (add, put, finish):
        loop(used, step)


def owners(labels):
    labels = labels.reshape(-1)
    ids = jnp.arange(labels.size, dtype=jnp.int32)
    owner = jnp.min(jnp.where(labels[:, None] == labels[None, :], ids[None, :], labels.size), axis=1)
    return labels, jnp.where(labels < 0, -1, owner)


def place(front, labels, owner, tiles, tile_rows):
    side = tiles.shape[2]
    size = labels.size
    smem, anyw = (pl.BlockSpec(memory_space=m) for m in (pltpu.SMEM, pl.ANY))
    return pl.pallas_call(
        functools.partial(place_kernel, tile_rows),
        grid=(1,),
        out_shape=jax.ShapeDtypeStruct(front.shape, f32),
        in_specs=[smem, smem, anyw, anyw],
        out_specs=anyw,
        input_output_aliases={3: 0},
        scratch_shapes=[
            pltpu.VMEM(tiles.shape, bf16),
            pltpu.VMEM((size, side, side), f32),
            pltpu.SMEM((size + 1,), jnp.int32),
            pltpu.SemaphoreType.DMA,
            pltpu.SemaphoreType.DMA((size,)),
            pltpu.SemaphoreType.DMA((size,)),
        ],
        compiler_params=pltpu.CompilerParams(vmem_limit_bytes=VMEM_LIMIT),
        name="place",
    )(labels, owner, tiles, front)


def bdot(a, b, dims):
    return lax.dot_general(a, b, (dims, ((), ())), precision=highest, preferred_element_type=f32)


STEP = 4


def eliminate(block):
    side = block.shape[0]
    lanes = lax.broadcasted_iota(jnp.int32, (1, side), 1)
    left = block
    right = jnp.where(
        lax.broadcasted_iota(jnp.int32, (side, side), 0) == lax.broadcasted_iota(jnp.int32, (side, side), 1), 1.0, 0.0
    )
    upper_rows, inverse_rows = [], []
    for k in range(0, side, STEP):
        base = k // 8 * 8
        cut = base - (side - left.shape[0])
        left, right = left[cut:], right[cut:]
        height = left.shape[0]
        wide = [jnp.broadcast_to(left[:, k + i : k + i + 1], (height, side)) for i in range(STEP)]
        cols, ups, invs = [], [], []
        for i in range(STEP):
            at = k + i - base
            col, up, inv = wide[i], left[at : at + 1], right[at : at + 1]
            for j in range(i):
                factor = cols[j][at : at + 1]
                col = col - cols[j] * factor
                up = up - ups[j] * factor
                inv = inv - invs[j] * factor
            scale = lax.rsqrt(col[at : at + 1])
            cols.append(col * scale)
            ups.append(up * scale)
            invs.append(inv * scale)
            upper_rows.append(jnp.where(lanes >= k + i, ups[i], 0.0))
            inverse_rows.append(invs[i])
        for i in range(STEP):
            left = left - cols[i] * ups[i]
            right = right - cols[i] * invs[i]
    return jnp.concatenate(upper_rows, axis=0), jnp.concatenate(inverse_rows, axis=0)


def decode_block(coded, lead):
    head = coded[lead:].astype(jnp.int32).astype(f32)[:, :lead]
    block = coded[:lead, :lead].astype(jnp.int32).astype(f32) * jnp.exp2(head[0:1])
    diagonal = (head[2:3] + head[3:4] * (1.0 / 32768.0)) * jnp.exp2(head[1:2])
    on = lax.broadcasted_iota(jnp.int32, block.shape, 0) == lax.broadcasted_iota(jnp.int32, block.shape, 1)
    return jnp.where(on, diagonal, block)


def factor(first, block, columns_ref, panel_ref, weights_ref):
    rows, lead = columns_ref.shape
    side = lead // 2
    eye = lax.broadcasted_iota(jnp.int32, (side, side), 0) == lax.broadcasted_iota(jnp.int32, (side, side), 1)
    b11, b21t, b22 = block[:side, :side], block[:side, side:], block[side:, side:]
    nt, nn = ((1,), (1,)), ((1,), (0,))
    up_one, inv_one = eliminate((b11 + b11.T) * 0.5)
    below = bdot(b21t.T, inv_one, nt)
    up_two, inv_two = eliminate((b22 + b22.T) * 0.5 - bdot(below, below, nt))
    corner = -bdot(inv_two, bdot(below, inv_one, nn), nn)
    left, right = columns_ref[:, :side], columns_ref[:, side:]
    panel_left = bdot(left, inv_one, nt)
    panel_right = bdot(left, corner, nt) + bdot(right, inv_two, nt)
    weight_left = bdot(panel_left, inv_one, nn) + bdot(panel_right, corner, nn)
    weight_right = bdot(panel_right, inv_two, nn)

    def put(low, cols, panel, weight):
        high = low + panel.shape[0]
        panel_ref[low:high, cols] = panel
        hi = weight.astype(bf16)
        weights_ref[low:high, cols] = hi
        weights_ref[rows + low : rows + high, cols] = (weight - hi.astype(f32)).astype(bf16)

    before, after = slice(0, side), slice(side, lead)
    put(0, before, panel_left, weight_left)
    put(0, after, panel_right, weight_right)

    @pl.when(first == 0)
    def _():
        one_eye, zero = jnp.where(eye, 1.0, 0.0), jnp.zeros((side, side), f32)
        put(0, before, up_one.T, one_eye)
        put(0, after, zero, zero)
        put(side, before, below, zero)
        put(side, after, up_two.T, one_eye)


def front_kernel(tile_rows, slots, starts, info_ref, labels_ref, columns_ref, tiles_ref, front_ref, *refs):
    count = len(starts) - 1
    parts, out_ref = refs[:count], refs[count]
    held, coded, weights, panel, in_sems, part_sems, out_sems = refs[count + 1 :]
    rows, lead = columns_ref.shape
    side = tiles_ref.shape[2]
    steps = starts[-1]
    part_copies = [
        pltpu.make_async_copy(part, coded.at[pl.ds(low, high - low)], part_sems.at[i])
        for i, (part, low, high) in enumerate(zip(parts, starts, starts[1:]))
    ]
    columns_of = lambda g: pl.ds(pl.multiple_of(g * rows, rows), rows)
    in_copies = [
        pltpu.make_async_copy(front_ref.at[:, columns_of(g)], held.at[:, columns_of(g)], in_sems.at[g])
        for g in range(steps)
    ]
    for copy in part_copies + in_copies:
        copy.start()
    for copy in part_copies:
        copy.wait()
    factor(info_ref[0], decode_block(coded[info_ref[1]], lead), columns_ref, panel, weights)
    for copy in in_copies:
        copy.wait()

    def add(n):
        d, s = n // FIRST, n % FIRST
        label = labels_ref[d * slots + s]
        q, col = label // tile_rows, label % tile_rows

        @pl.when((label >= 0) & (col >= 2))
        def _():
            at = (pl.ds(pl.multiple_of(q * side, side), side),
                  pl.ds(pl.multiple_of(col * side, side), side))
            held[at] = held[at] + tiles_ref[d, pl.ds(pl.multiple_of(s * side, side), side)].astype(f32)

    loop(tiles_ref.shape[0] * FIRST, add)
    dot = functools.partial(jnp.dot, preferred_element_type=f32)

    def out_copy(g):
        at = columns_of(info_ref[2 + g])
        return pltpu.make_async_copy(held.at[:, at], out_ref.at[:, at], out_sems.at[g])

    def step(g):
        block = info_ref[2 + g]
        values = coded[g, :lead].astype(jnp.int32)
        scale = jnp.exp2(coded[g, lead:].astype(jnp.int32).astype(f32)[0:1])
        lower = ((values + 128) & 255) - 128
        hi = (values - lower).astype(f32).astype(bf16)
        lo = lower.astype(f32).astype(bf16)
        both = dot(weights[...], hi)
        total = both[:rows] + both[rows:] + dot(weights[:rows], lo)
        held[:, columns_of(block)] = held[:, columns_of(block)] - total * scale

        @pl.when(block == 0)
        def _():
            held[:, :lead] = panel[...]

        out_copy(g).start()

    loop(steps, step)
    loop(steps, lambda g: out_copy(g).wait())


def make_front(info, labels, columns, arrived, frontal, parts, tile_rows):
    rows, order = frontal.shape
    lead = columns.shape[1]
    starts = [0]
    for part in parts:
        starts.append(starts[-1] + part.shape[0])
    smem, anyw = (pl.BlockSpec(memory_space=m) for m in (pltpu.SMEM, pl.ANY))
    return pl.pallas_call(
        functools.partial(front_kernel, tile_rows, labels.shape[1], tuple(starts)),
        grid=(1,),
        out_shape=jax.ShapeDtypeStruct((rows, order), f32),
        in_specs=[
            smem, smem,
            pl.BlockSpec((rows, lead), lambda i: (0, 0)),
            pl.BlockSpec(arrived.shape, lambda i: (0, 0, 0)),
            anyw,
        ] + [anyw] * len(parts),
        out_specs=anyw,
        scratch_shapes=[
            pltpu.VMEM((rows, order), f32),
            pltpu.VMEM((starts[-1], lead + HEAD, rows), jnp.int16),
            pltpu.VMEM((2 * rows, lead), bf16),
            pltpu.VMEM((rows, lead), f32),
            pltpu.SemaphoreType.DMA((starts[-1],)),
            pltpu.SemaphoreType.DMA((len(parts),)),
            pltpu.SemaphoreType.DMA((starts[-1],)),
        ],
        compiler_params=pltpu.CompilerParams(vmem_limit_bytes=VMEM_LIMIT),
        cost_estimate=pl.CostEstimate(
            flops=6 * rows * order * lead, bytes_accessed=8 * rows * order, transcendentals=0
        ),
        name="front",
    )(info, labels.reshape(-1), columns, arrived, frontal, *parts)


def local_fast(frontal, child_tiles, child_rows, child_cols):
    rows, order = frontal.shape
    side = child_tiles.shape[1]
    lead = 2 * side
    tile_rows = order // side
    devices = lax.axis_size("row")
    layers = devices // 4
    slots = MOST_SAME * rows // side
    row = lax.axis_index("row").astype(jnp.int32)
    every = [(z, x, c) for z in range(layers) for x in range(2) for c in range(2)]
    index = lambda z, x, c: z % layers * 4 + x * 2 + c
    over_core = [(index(z, x, c), index(z, x, 1 - c)) for z, x, c in every]
    over_x = [(index(z, x, c), index(z, 1 - x, c)) for z, x, c in every]
    over_z = lambda s: [(index(z, x, c), index(z + s, x, c)) for z, x, c in every]
    send = lambda x, pairs: lax.ppermute(x, "row", pairs)
    exchange = lambda x: lax.all_to_all(x, "row", split_axis=0, concat_axis=0, tiled=True)

    first, second, third = pack(child_tiles, child_rows, child_cols, devices, tile_rows)
    one = exchange(first)
    head = one[:, FIRST * side : FIRST * side + 2, :slots].astype(f32)
    labels = head[:, 0].astype(jnp.int32) - 1
    columns, narrow = lead_columns(row[None], labels, frontal, one, tile_rows)

    z, x, c = row // 4, row // 2 % 2, row % 2
    cols = []
    for offsets in ([0], [1, layers - 1], list(range(2, layers - 1))):
        cols += [
            (z - dz) % layers * 4 + (x ^ dx) * 2 + (c ^ dc) for dc in range(2) for dx in range(2) for dz in offsets
        ]
    at = sum(jnp.where(col == 0, g, 0) for g, col in enumerate(cols))
    info = jnp.stack([row, at] + cols).astype(jnp.int32)
    wanted = jnp.where(labels % tile_rows < 2, -1, labels)
    spots = owners(wanted[:, FIRST : FIRST + SECOND])
    flags = jnp.max(head[:, 1, :2], axis=0)
    flags = jnp.maximum(flags, lax.ppermute(flags, "groups", [(0, 1), (1, 0)]))
    case = jnp.where(flags[0] > 0, 2, jnp.where(flags[1] > 0, 1, 0)).astype(jnp.int32)

    join = lambda *x: jnp.concatenate(x, axis=0)
    tie = lax.optimization_barrier
    narrow, second = tie((narrow, second))
    up, down, over = send(narrow, over_z(1)), send(narrow, over_z(layers - 1)), send(narrow, over_x)
    narrow, up, down, over = tie((narrow, up, down, over))
    near, beside = join(narrow, over), join(up, down)
    far = [send(narrow, over_z(s)) for s in range(2, layers - 1)]
    beside_x, near_c = send(beside, over_x), send(near, over_core)
    far, beside_x, near_c, near, beside, info, spots, case = tie(
        (far, beside_x, near_c, near, beside, info, spots, case)
    )
    far, beside = join(*far), join(beside, beside_x)
    far_x, beside_c = send(far, over_x), send(beside, over_core)
    far_x, beside_c, far = tie((far_x, beside_c, far))
    far = join(far, far_x)
    far_c = send(far, over_core)
    far_c, second = tie((far_c, second))
    two = exchange(second)
    parts = [near, near_c, beside, beside_c, far, far_c]
    front = make_front(info, labels, columns, one, frontal, parts, tile_rows)
    front, two = tie((front, two))
    front = place(front, *spots, two, tile_rows)
    front, third, wanted = tie((front, third, wanted[:, FIRST + SECOND :]))

    def spread(x, axis):
        every = exchange(jnp.broadcast_to(x[None], (devices,) + x.shape))
        return every.reshape(order, x.shape[1])

    return lax.switch(
        case,
        [
            lambda front, third, wanted, *args: front,
            lambda front, third, wanted, *args: place(front, *owners(wanted), exchange(third), tile_rows),
            lambda front, third, wanted, *args: local_small(*args, spread),
        ],
        front, third, wanted, frontal, child_tiles, child_rows, child_cols,
    )


def gather_rows(x, axis):
    return lax.all_gather(x, axis, axis=0, tiled=True)


def factor_rows(column_block, square_block, low_edge):
    tile_side = square_block.shape[0]
    factor = jnp.linalg.cholesky(square_block)
    identity = jnp.eye(tile_side, dtype=column_block.dtype)
    inverse = jax.scipy.linalg.solve_triangular(factor, identity, lower=True)
    solved = jnp.dot(column_block, inverse.T, precision=highest)
    row_ids = jnp.arange(column_block.shape[0], dtype=jnp.int32)
    inside = (row_ids >= low_edge) & (row_ids < low_edge + tile_side)
    within = jnp.take(factor, jnp.clip(row_ids - low_edge, 0, tile_side - 1), axis=0)
    before = row_ids < low_edge
    return jnp.where(
        inside[:, None], within, jnp.where(before[:, None], jnp.zeros_like(solved), solved)
    )


def apply_panel(current, panel_rows, update, low_edge):
    tile_side = panel_rows.shape[1]
    col_ids = jnp.arange(current.shape[1], dtype=jnp.int32)[None, :]
    current = jnp.where(col_ids >= low_edge + tile_side, current - update, current)
    return current.at[:, low_edge : low_edge + tile_side].set(panel_rows)


def pack_pieces(child_tiles, child_rows, child_cols, selected, rows_dev, order):
    tile_total = child_tiles.shape[0]
    tile_side = child_tiles.shape[1]
    tile_rows = order // tile_side
    piece_rows = min(rows_dev, tile_side)
    per_tile = tile_side // piece_rows
    capacity = MOST_SAME * max(1, rows_dev // tile_side)
    devices = lax.axis_size("row")
    parent = child_rows[:, 0]
    grouping = parent * tile_side // max(rows_dev, tile_side)
    sequence = jnp.arange(tile_total, dtype=jnp.int32)
    earlier = (
        (grouping[:, None] == grouping[None, :])
        & (sequence[None, :] < sequence[:, None])
        & selected[None, :]
    )
    slot_ids = jnp.sum(earlier.astype(jnp.int32), axis=1)
    offsets = (
        parent[:, None] * tile_side + jnp.arange(per_tile, dtype=jnp.int32)[None, :] * piece_rows
    )
    targets = jnp.where(selected[:, None], offsets // rows_dev, devices)
    local_ids = offsets % rows_dev // piece_rows
    slot_grid = jnp.broadcast_to(slot_ids[:, None], targets.shape)
    pieces = child_tiles.reshape(tile_total, per_tile, piece_rows, tile_side)
    outgoing = (
        jnp.zeros((devices, capacity, piece_rows, tile_side), child_tiles.dtype)
        .at[targets, slot_grid]
        .set(pieces, mode="drop")
    )
    position = local_ids * tile_rows + child_cols[:, None]
    labels = (
        jnp.full((devices, capacity), -1, jnp.int32)
        .at[targets, slot_grid]
        .set(position, mode="drop")
    )
    return (outgoing, labels)


def place_pieces(arrived, arrived_ids, rows_dev, order):
    piece_rows = arrived.shape[2]
    tile_side = arrived.shape[3]
    tile_rows = order // tile_side
    blocks_dev = rows_dev // piece_rows
    count = arrived.shape[0] * arrived.shape[1]
    selector = (
        arrived_ids.reshape(-1, 1) == jnp.arange(blocks_dev * tile_rows, dtype=jnp.int32)[None, :]
    ).astype(arrived.dtype)
    selector = selector.reshape(count, blocks_dev, tile_rows)
    flattened = arrived.reshape(count, piece_rows, tile_side)
    assembled_part = jnp.einsum(
        "nqc,nsw->qscw", selector, flattened, preferred_element_type=jnp.float32
    )
    return assembled_part.reshape(rows_dev, order)


def local_small(frontal, child_tiles, child_rows, child_cols, gather):
    rows_dev = frontal.shape[0]
    order = frontal.shape[1]
    tile_side = child_tiles.shape[1]
    first_row = lax.axis_index("row") * rows_dev
    current = frontal
    everything = jnp.ones(child_cols.shape, dtype=bool)
    outgoing, labels = pack_pieces(child_tiles, child_rows, child_cols, everything, rows_dev, order)
    arrived, arrived_ids = (
        lax.all_to_all(outgoing, "row", split_axis=0, concat_axis=0, tiled=True),
        lax.all_to_all(labels, "row", split_axis=0, concat_axis=0, tiled=True),
    )
    current = current + place_pieces(arrived, arrived_ids, rows_dev, order)
    leading = gather(current[:, : 2 * tile_side], "row")
    first_all = factor_rows(leading[:, :tile_side], leading[:tile_side, :tile_side], 0)
    second_block = leading[:, tile_side:] - jnp.dot(
        first_all, first_all[tile_side : 2 * tile_side].T, precision=highest
    )
    second_all = factor_rows(second_block, second_block[tile_side : 2 * tile_side], tile_side)
    for panel_index, panel_all in enumerate((first_all, second_all)):
        low_edge = panel_index * tile_side
        panel_own = lax.dynamic_slice_in_dim(panel_all, first_row, rows_dev, 0)
        update = jnp.dot(panel_own, panel_all.T, precision=highest)
        current = apply_panel(current, panel_own, update, low_edge)
    return current


def local(frontal, child_tiles, child_rows, child_cols):
    rows, order = frontal.shape
    side = child_tiles.shape[1]
    devices = lax.axis_size("row")
    wide = rows >= 2 * side and rows % side == 0 and MOST_SAME * rows // side > FIRST + SECOND
    if wide and order == devices * rows and devices % 4 == 0 and devices >= 16 and lax.axis_size("groups") == 2:
        return local_fast(frontal, child_tiles, child_rows, child_cols)
    return local_small(frontal, child_tiles, child_rows, child_cols, gather_rows)


def solution(mesh):
    return jax.shard_map(
        local,
        mesh=mesh,
        in_specs=(
            P(("groups", "row"), None),
            P(("groups", "row"), None, None),
            P(("groups", "row"), None),
            P(("groups", "row")),
        ),
        out_specs=P(("groups", "row"), None),
        check_vma=False,
    )
```

```python
import functools
import jax
import jax.numpy as jnp
from jax import lax
from jax.experimental import pallas as pl
from jax.experimental.pallas import tpu as pltpu
from jax.sharding import PartitionSpec as P

MOST_SAME = 2
FIRST = 3
SECOND = 3
HEAD = 16
VMEM_LIMIT = 56 << 20


highest = lax.Precision.HIGHEST
f32, bf16 = jnp.float32, jnp.bfloat16


def loop(count, body, unroll=1):
    lax.fori_loop(0, count, lambda i, carry: (body(i), carry)[1], 0, unroll=unroll)


def pack_kernel(
    tile_rows, per_dev, rows_ref, cols_ref, tiles_ref, first_ref, second_ref, third_ref,
    heads, heads_out, counts, sem, head_sem,
):
    tiles, side, _ = tiles_ref.shape
    devices = first_ref.shape[0]
    lanes = lax.broadcasted_iota(jnp.int32, (8, 128), 1)
    subs = lax.broadcasted_iota(jnp.int32, (8, 128), 0)
    heads[...] = jnp.zeros_like(heads)

    def clear(d):
        counts[d] = 0

    loop(devices, clear)

    def place(i, wanted):
        row, col = rows_ref[i], cols_ref[i]

        @pl.when((col < 2) == wanted)
        def _():
            d, q = row // per_dev, row % per_dev
            s = counts[d]
            counts[d] = s + 1
            here = (lanes == s) & (subs == 0)
            heads[d] = jnp.where(here, (q * tile_rows + col + 1).astype(f32), heads[d])

            @pl.when(s < FIRST)
            def _():
                pltpu.make_async_copy(
                    tiles_ref.at[i], first_ref.at[d, pl.ds(s * side, side)], sem
                ).start()

            @pl.when((s >= FIRST) & (s < FIRST + SECOND))
            def _():
                pltpu.make_async_copy(
                    tiles_ref.at[i], second_ref.at[d, pl.ds((s - FIRST) * side, side)], sem
                ).start()

            @pl.when(s >= FIRST + SECOND)
            def _():
                pltpu.make_async_copy(
                    tiles_ref.at[i],
                    third_ref.at[d, pl.ds((s - FIRST - SECOND) * side, side)],
                    sem,
                ).start()

    def most():
        return lax.fori_loop(0, devices, lambda d, m: jnp.maximum(m, counts[d]), 0)

    loop(tiles, lambda i: place(i, True), 4)
    lead_most = most().astype(f32)
    loop(tiles, lambda i: place(i, False), 4)
    flags = jnp.where(lanes == 0, lead_most, jnp.where(lanes == 1, most().astype(f32), 0.0))
    marked = jnp.where((subs == 1)[None], flags[None], heads[...])
    heads_out[...] = jnp.concatenate([marked, jnp.zeros_like(marked)], axis=1).astype(bf16)
    copy = pltpu.make_async_copy(heads_out, first_ref.at[:, pl.ds(FIRST * side, HEAD)], head_sem)
    copy.start()

    pltpu.make_async_copy(tiles_ref, tiles_ref, sem).wait()
    copy.wait()


def pack(child_tiles, child_rows, child_cols, devices, tile_rows):
    tiles, side, _ = child_tiles.shape
    per_dev = tile_rows // devices
    third = MOST_SAME * per_dev - FIRST - SECOND
    smem, anyw = (pl.BlockSpec(memory_space=m) for m in (pltpu.SMEM, pl.ANY))
    return pl.pallas_call(
        functools.partial(pack_kernel, tile_rows, per_dev),
        grid=(1,),
        out_shape=(
            jax.ShapeDtypeStruct((devices, FIRST * side + HEAD, side), bf16),
            jax.ShapeDtypeStruct((devices, SECOND * side, side), bf16),
            jax.ShapeDtypeStruct((devices, third * side, side), bf16),
        ),
        in_specs=[smem, smem, pl.BlockSpec((tiles, side, side), lambda i: (0, 0, 0))],
        out_specs=(anyw, anyw, anyw),
        scratch_shapes=[
            pltpu.VMEM((devices, 8, 128), f32),
            pltpu.VMEM((devices, HEAD, 128), bf16),
            pltpu.SMEM((devices,), jnp.int32),
            pltpu.SemaphoreType.DMA,
            pltpu.SemaphoreType.DMA,
        ],
        compiler_params=pltpu.CompilerParams(vmem_limit_bytes=VMEM_LIMIT),
        name="pack",
    )(child_rows[:, 0], child_cols, child_tiles)


def lead_kernel(tile_rows, slots, row_ref, labels_ref, front_ref, tiles_ref, out_ref, coded_ref):
    side = tiles_ref.shape[2]
    rows, lead = out_ref.shape
    out_ref[...] = front_ref[...]

    def body(n):
        d, s = n // FIRST, n % FIRST
        label = labels_ref[d * slots + s]
        q, col = label // tile_rows, label % tile_rows

        @pl.when((label >= 0) & (col < 2))
        def _():
            at = (pl.ds(pl.multiple_of(q * side, side), side),
                  pl.ds(pl.multiple_of(col * side, side), side))
            out_ref[at] = out_ref[at] + tiles_ref[d, pl.ds(pl.multiple_of(s * side, side), side)].astype(f32)

    loop(tiles_ref.shape[0] * FIRST, body)
    low, high = -32768.0, 32767.0
    turned = out_ref[...].T
    on = lax.broadcasted_iota(jnp.int32, turned.shape, 0) == lax.broadcasted_iota(jnp.int32, turned.shape, 1)
    diagonal = jnp.sum(jnp.where(on, turned, 0.0), axis=0, keepdims=True)
    turned = jnp.where(on & (row_ref[0] == 0), 0.0, turned)

    def power(most):
        return jnp.ceil(jnp.log2(jnp.maximum(most, 1e-30))) - 15.0

    scale = power(jnp.max(jnp.abs(turned), axis=0, keepdims=True))
    values = jnp.clip(jnp.round(turned * jnp.exp2(-scale)), low, high)
    coded_ref[0, :lead] = values.astype(jnp.int32).astype(jnp.int16)
    own = power(jnp.abs(diagonal))
    wide = diagonal * jnp.exp2(-own)
    upper = jnp.clip(jnp.round(wide), low, high)
    lower = jnp.clip(jnp.round((wide - upper) * 32768.0), low, high)
    subs = lax.broadcasted_iota(jnp.int32, (HEAD, rows), 0)
    head = jnp.zeros((HEAD, rows), f32)
    for i, value in enumerate((scale, own, upper, lower)):
        head = jnp.where(subs == i, value, head)
    coded_ref[0, lead:] = head.astype(jnp.int32).astype(jnp.int16)


def lead_columns(row, labels, frontal, arrived, tile_rows):
    rows = frontal.shape[0]
    lead = 2 * arrived.shape[2]
    smem = pl.BlockSpec(memory_space=pltpu.SMEM)
    return pl.pallas_call(
        functools.partial(lead_kernel, tile_rows, labels.shape[1]),
        grid=(1,),
        out_shape=(
            jax.ShapeDtypeStruct((rows, lead), f32),
            jax.ShapeDtypeStruct((1, lead + HEAD, rows), jnp.int16),
        ),
        in_specs=[
            smem, smem,
            pl.BlockSpec((rows, lead), lambda i: (0, 0)),
            pl.BlockSpec(arrived.shape, lambda i: (0, 0, 0)),
        ],
        out_specs=(
            pl.BlockSpec((rows, lead), lambda i: (0, 0)),
            pl.BlockSpec((1, lead + HEAD, rows), lambda i: (0, 0, 0)),
        ),
        compiler_params=pltpu.CompilerParams(vmem_limit_bytes=VMEM_LIMIT),
        name="lead_columns",
    )(row, labels.reshape(-1), frontal, arrived)


def place_kernel(
    tile_rows, labels_ref, owner_ref, arrived_ref, front_ref, out_ref, tiles_ref, held, listed, tile_sem, in_sems, out_sems
):
    side = tiles_ref.shape[2]
    slots = tiles_ref.shape[1] // side
    tile_copy = pltpu.make_async_copy(arrived_ref, tiles_ref, tile_sem)
    tile_copy.start()

    def spot(n):
        label = labels_ref[n]
        q, col = label // tile_rows, label % tile_rows
        return out_ref.at[pl.ds(pl.multiple_of(q * side, side), side), pl.ds(pl.multiple_of(col * side, side), side)]

    def fetch(n, used):
        listed[used] = n

        @pl.when(owner_ref[n] == n)
        def _():
            pltpu.make_async_copy(spot(n), held.at[n], in_sems.at[n]).start()

        return used + (labels_ref[n] >= 0).astype(jnp.int32)

    def add(i):
        n = listed[i]
        m = owner_ref[n]

        @pl.when(m == n)
        def _():
            pltpu.make_async_copy(spot(n), held.at[n], in_sems.at[n]).wait()

        held[m] += tiles_ref[n // slots, pl.ds(pl.multiple_of(n % slots * side, side), side)].astype(f32)

    def put(i):
        n = listed[i]

        @pl.when(owner_ref[n] == n)
        def _():
            pltpu.make_async_copy(held.at[n], spot(n), out_sems.at[n]).start()

    def finish(i):
        n = listed[i]

        @pl.when(owner_ref[n] == n)
        def _():
            pltpu.make_async_copy(held.at[n], spot(n), out_sems.at[n]).wait()

    used = lax.fori_loop(0, tiles_ref.shape[0] * slots, fetch, 0, unroll=4)
    tile_copy.wait()
    for step in (add, put, finish):
        loop(used, step)


def owners(labels):
    labels = labels.reshape(-1)
    ids = jnp.arange(labels.size, dtype=jnp.int32)
    owner = jnp.min(jnp.where(labels[:, None] == labels[None, :], ids[None, :], labels.size), axis=1)
    return labels, jnp.where(labels < 0, -1, owner)


def place(front, labels, owner, tiles, tile_rows):
    side = tiles.shape[2]
    size = labels.size
    smem, anyw = (pl.BlockSpec(memory_space=m) for m in (pltpu.SMEM, pl.ANY))
    return pl.pallas_call(
        functools.partial(place_kernel, tile_rows),
        grid=(1,),
        out_shape=jax.ShapeDtypeStruct(front.shape, f32),
        in_specs=[smem, smem, anyw, anyw],
        out_specs=anyw,
        input_output_aliases={3: 0},
        scratch_shapes=[
            pltpu.VMEM(tiles.shape, bf16),
            pltpu.VMEM((size, side, side), f32),
            pltpu.SMEM((size + 1,), jnp.int32),
            pltpu.SemaphoreType.DMA,
            pltpu.SemaphoreType.DMA((size,)),
            pltpu.SemaphoreType.DMA((size,)),
        ],
        compiler_params=pltpu.CompilerParams(vmem_limit_bytes=VMEM_LIMIT),
        name="place",
    )(labels, owner, tiles, front)


def bdot(a, b, dims):
    return lax.dot_general(a, b, (dims, ((), ())), precision=highest, preferred_element_type=f32)


STEP = 4


def eliminate(block):
    side = block.shape[0]
    lanes = lax.broadcasted_iota(jnp.int32, (1, side), 1)
    left = block
    right = jnp.where(
        lax.broadcasted_iota(jnp.int32, (side, side), 0) == lax.broadcasted_iota(jnp.int32, (side, side), 1), 1.0, 0.0
    )
    upper_rows, inverse_rows = [], []
    for k in range(0, side, STEP):
        base = k // 8 * 8
        cut = base - (side - left.shape[0])
        left, right = left[cut:], right[cut:]
        height = left.shape[0]
        wide = [jnp.broadcast_to(left[:, k + i : k + i + 1], (height, side)) for i in range(STEP)]
        cols, ups, invs = [], [], []
        for i in range(STEP):
            at = k + i - base
            col, up, inv = wide[i], left[at : at + 1], right[at : at + 1]
            for j in range(i):
                factor = cols[j][at : at + 1]
                col = col - cols[j] * factor
                up = up - ups[j] * factor
                inv = inv - invs[j] * factor
            scale = lax.rsqrt(col[at : at + 1])
            cols.append(col * scale)
            ups.append(up * scale)
            invs.append(inv * scale)
            upper_rows.append(jnp.where(lanes >= k + i, ups[i], 0.0))
            inverse_rows.append(invs[i])
        for i in range(STEP):
            left = left - cols[i] * ups[i]
            right = right - cols[i] * invs[i]
    return jnp.concatenate(upper_rows, axis=0), jnp.concatenate(inverse_rows, axis=0)


def decode_block(coded, lead):
    head = coded[lead:].astype(jnp.int32).astype(f32)[:, :lead]
    block = coded[:lead, :lead].astype(jnp.int32).astype(f32) * jnp.exp2(head[0:1])
    diagonal = (head[2:3] + head[3:4] * (1.0 / 32768.0)) * jnp.exp2(head[1:2])
    on = lax.broadcasted_iota(jnp.int32, block.shape, 0) == lax.broadcasted_iota(jnp.int32, block.shape, 1)
    return jnp.where(on, diagonal, block)


def factor(first, block, columns_ref, panel_ref, weights_ref):
    rows, lead = columns_ref.shape
    side = lead // 2
    eye = lax.broadcasted_iota(jnp.int32, (side, side), 0) == lax.broadcasted_iota(jnp.int32, (side, side), 1)
    b11, b21t, b22 = block[:side, :side], block[:side, side:], block[side:, side:]
    nt, nn = ((1,), (1,)), ((1,), (0,))
    up_one, inv_one = eliminate((b11 + b11.T) * 0.5)
    below = bdot(b21t.T, inv_one, nt)
    up_two, inv_two = eliminate((b22 + b22.T) * 0.5 - bdot(below, below, nt))
    corner = -bdot(inv_two, bdot(below, inv_one, nn), nn)
    left, right = columns_ref[:, :side], columns_ref[:, side:]
    panel_left = bdot(left, inv_one, nt)
    panel_right = bdot(left, corner, nt) + bdot(right, inv_two, nt)
    weight_left = bdot(panel_left, inv_one, nn) + bdot(panel_right, corner, nn)
    weight_right = bdot(panel_right, inv_two, nn)

    def put(low, cols, panel, weight):
        high = low + panel.shape[0]
        panel_ref[low:high, cols] = panel
        hi = weight.astype(bf16)
        weights_ref[low:high, cols] = hi
        weights_ref[rows + low : rows + high, cols] = (weight - hi.astype(f32)).astype(bf16)

    before, after = slice(0, side), slice(side, lead)
    put(0, before, panel_left, weight_left)
    put(0, after, panel_right, weight_right)

    @pl.when(first == 0)
    def _():
        one_eye, zero = jnp.where(eye, 1.0, 0.0), jnp.zeros((side, side), f32)
        put(0, before, up_one.T, one_eye)
        put(0, after, zero, zero)
        put(side, before, below, zero)
        put(side, after, up_two.T, one_eye)


def front_kernel(tile_rows, slots, starts, info_ref, labels_ref, columns_ref, tiles_ref, front_ref, *refs):
    count = len(starts) - 1
    parts, out_ref = refs[:count], refs[count]
    held, coded, weights, panel, in_sems, part_sems, out_sems = refs[count + 1 :]
    rows, lead = columns_ref.shape
    side = tiles_ref.shape[2]
    steps = starts[-1]
    part_copies = [
        pltpu.make_async_copy(part, coded.at[pl.ds(low, high - low)], part_sems.at[i])
        for i, (part, low, high) in enumerate(zip(parts, starts, starts[1:]))
    ]
    columns_of = lambda g: pl.ds(pl.multiple_of(g * rows, rows), rows)
    in_copies = [
        pltpu.make_async_copy(front_ref.at[:, columns_of(g)], held.at[:, columns_of(g)], in_sems.at[g])
        for g in range(steps)
    ]
    for copy in part_copies + in_copies:
        copy.start()
    for copy in part_copies:
        copy.wait()
    factor(info_ref[0], decode_block(coded[info_ref[1]], lead), columns_ref, panel, weights)
    for copy in in_copies:
        copy.wait()

    def add(n):
        d, s = n // FIRST, n % FIRST
        label = labels_ref[d * slots + s]
        q, col = label // tile_rows, label % tile_rows

        @pl.when((label >= 0) & (col >= 2))
        def _():
            at = (pl.ds(pl.multiple_of(q * side, side), side),
                  pl.ds(pl.multiple_of(col * side, side), side))
            held[at] = held[at] + tiles_ref[d, pl.ds(pl.multiple_of(s * side, side), side)].astype(f32)

    loop(tiles_ref.shape[0] * FIRST, add)
    dot = functools.partial(jnp.dot, preferred_element_type=f32)

    def out_copy(g):
        at = columns_of(info_ref[2 + g])
        return pltpu.make_async_copy(held.at[:, at], out_ref.at[:, at], out_sems.at[g])

    def step(g):
        block = info_ref[2 + g]
        values = coded[g, :lead].astype(jnp.int32)
        scale = jnp.exp2(coded[g, lead:].astype(jnp.int32).astype(f32)[0:1])
        lower = ((values + 128) & 255) - 128
        hi = (values - lower).astype(f32).astype(bf16)
        lo = lower.astype(f32).astype(bf16)
        both = dot(weights[...], hi)
        total = both[:rows] + both[rows:] + dot(weights[:rows], lo)
        held[:, columns_of(block)] = held[:, columns_of(block)] - total * scale

        @pl.when(block == 0)
        def _():
            held[:, :lead] = panel[...]

        out_copy(g).start()

    loop(steps, step)
    loop(steps, lambda g: out_copy(g).wait())


def make_front(info, labels, columns, arrived, frontal, parts, tile_rows):
    rows, order = frontal.shape
    lead = columns.shape[1]
    starts = [0]
    for part in parts:
        starts.append(starts[-1] + part.shape[0])
    smem, anyw = (pl.BlockSpec(memory_space=m) for m in (pltpu.SMEM, pl.ANY))
    return pl.pallas_call(
        functools.partial(front_kernel, tile_rows, labels.shape[1], tuple(starts)),
        grid=(1,),
        out_shape=jax.ShapeDtypeStruct((rows, order), f32),
        in_specs=[
            smem, smem,
            pl.BlockSpec((rows, lead), lambda i: (0, 0)),
            pl.BlockSpec(arrived.shape, lambda i: (0, 0, 0)),
            anyw,
        ] + [anyw] * len(parts),
        out_specs=anyw,
        scratch_shapes=[
            pltpu.VMEM((rows, order), f32),
            pltpu.VMEM((starts[-1], lead + HEAD, rows), jnp.int16),
            pltpu.VMEM((2 * rows, lead), bf16),
            pltpu.VMEM((rows, lead), f32),
            pltpu.SemaphoreType.DMA((starts[-1],)),
            pltpu.SemaphoreType.DMA((len(parts),)),
            pltpu.SemaphoreType.DMA((starts[-1],)),
        ],
        compiler_params=pltpu.CompilerParams(vmem_limit_bytes=VMEM_LIMIT),
        cost_estimate=pl.CostEstimate(
            flops=6 * rows * order * lead, bytes_accessed=8 * rows * order, transcendentals=0
        ),
        name="front",
    )(info, labels.reshape(-1), columns, arrived, frontal, *parts)


def local_fast(frontal, child_tiles, child_rows, child_cols):
    rows, order = frontal.shape
    side = child_tiles.shape[1]
    lead = 2 * side
    tile_rows = order // side
    devices = lax.axis_size("row")
    layers = devices // 4
    slots = MOST_SAME * rows // side
    row = lax.axis_index("row").astype(jnp.int32)
    every = [(z, x, c) for z in range(layers) for x in range(2) for c in range(2)]
    index = lambda z, x, c: z % layers * 4 + x * 2 + c
    over_core = [(index(z, x, c), index(z, x, 1 - c)) for z, x, c in every]
    over_x = [(index(z, x, c), index(z, 1 - x, c)) for z, x, c in every]
    over_z = lambda s: [(index(z, x, c), index(z + s, x, c)) for z, x, c in every]
    send = lambda x, pairs: lax.ppermute(x, "row", pairs)
    exchange = lambda x: lax.all_to_all(x, "row", split_axis=0, concat_axis=0, tiled=True)

    first, second, third = pack(child_tiles, child_rows, child_cols, devices, tile_rows)
    one = exchange(first)
    head = one[:, FIRST * side : FIRST * side + 2, :slots].astype(f32)
    labels = head[:, 0].astype(jnp.int32) - 1
    columns, narrow = lead_columns(row[None], labels, frontal, one, tile_rows)

    z, x, c = row // 4, row // 2 % 2, row % 2
    cols = []
    for offsets in ([0], [1, layers - 1], list(range(2, layers - 1))):
        cols += [
            (z - dz) % layers * 4 + (x ^ dx) * 2 + (c ^ dc) for dc in range(2) for dx in range(2) for dz in offsets
        ]
    at = sum(jnp.where(col == 0, g, 0) for g, col in enumerate(cols))
    info = jnp.stack([row, at] + cols).astype(jnp.int32)
    wanted = jnp.where(labels % tile_rows < 2, -1, labels)
    spots = owners(wanted[:, FIRST : FIRST + SECOND])
    flags = jnp.max(head[:, 1, :2], axis=0)
    flags = jnp.maximum(flags, lax.ppermute(flags, "groups", [(0, 1), (1, 0)]))
    case = jnp.where(flags[0] > FIRST, 2, jnp.where(flags[1] > FIRST + SECOND, 1, 0)).astype(jnp.int32)
    more = flags[1] > FIRST + SECOND + 1

    join = lambda *x: jnp.concatenate(x, axis=0)
    tie = lax.optimization_barrier
    narrow, second = tie((narrow, second))
    up, down, over = send(narrow, over_z(1)), send(narrow, over_z(layers - 1)), send(narrow, over_x)
    narrow, up, down, over = tie((narrow, up, down, over))
    near, beside = join(narrow, over), join(up, down)
    far = [send(narrow, over_z(s)) for s in range(2, layers - 1)]
    beside_x, near_c = send(beside, over_x), send(near, over_core)
    far, beside_x, near_c, near, beside, info, spots, case, more = tie(
        (far, beside_x, near_c, near, beside, info, spots, case, more)
    )
    far, beside = join(*far), join(beside, beside_x)
    far_x, beside_c = send(far, over_x), send(beside, over_core)
    far_x, beside_c, far = tie((far_x, beside_c, far))
    far = join(far, far_x)
    far_c = send(far, over_core)
    far_c, second = tie((far_c, second))
    two = exchange(second)
    parts = [near, near_c, beside, beside_c, far, far_c]
    front = make_front(info, labels, columns, one, frontal, parts, tile_rows)
    front, two = tie((front, two))
    front = place(front, *spots, two, tile_rows)
    front, third, wanted = tie((front, third, wanted[:, FIRST + SECOND :]))

    def spread(x, axis):
        every = exchange(jnp.broadcast_to(x[None], (devices,) + x.shape))
        return every.reshape(order, x.shape[1])

    def place_third(front, third, wanted, more, *args):
        front = place(front, *owners(wanted[:, :1]), exchange(third[:, :side]), tile_rows)
        if third.shape[1] == side:
            return front
        return lax.cond(
            more,
            lambda front: place(front, *owners(wanted[:, 1:]), exchange(third[:, side:]), tile_rows),
            lambda front: front,
            front,
        )

    return lax.switch(
        case,
        [
            lambda front, *args: front,
            place_third,
            lambda front, third, wanted, more, *args: local_small(*args, spread),
        ],
        front, third, wanted, more, frontal, child_tiles, child_rows, child_cols,
    )


def gather_rows(x, axis):
    return lax.all_gather(x, axis, axis=0, tiled=True)


def factor_rows(column_block, square_block, low_edge):
    tile_side = square_block.shape[0]
    factor = jnp.linalg.cholesky(square_block)
    identity = jnp.eye(tile_side, dtype=column_block.dtype)
    inverse = jax.scipy.linalg.solve_triangular(factor, identity, lower=True)
    solved = jnp.dot(column_block, inverse.T, precision=highest)
    row_ids = jnp.arange(column_block.shape[0], dtype=jnp.int32)
    inside = (row_ids >= low_edge) & (row_ids < low_edge + tile_side)
    within = jnp.take(factor, jnp.clip(row_ids - low_edge, 0, tile_side - 1), axis=0)
    before = row_ids < low_edge
    return jnp.where(
        inside[:, None], within, jnp.where(before[:, None], jnp.zeros_like(solved), solved)
    )


def apply_panel(current, panel_rows, update, low_edge):
    tile_side = panel_rows.shape[1]
    col_ids = jnp.arange(current.shape[1], dtype=jnp.int32)[None, :]
    current = jnp.where(col_ids >= low_edge + tile_side, current - update, current)
    return current.at[:, low_edge : low_edge + tile_side].set(panel_rows)


def pack_pieces(child_tiles, child_rows, child_cols, selected, rows_dev, order):
    tile_total = child_tiles.shape[0]
    tile_side = child_tiles.shape[1]
    tile_rows = order // tile_side
    piece_rows = min(rows_dev, tile_side)
    per_tile = tile_side // piece_rows
    capacity = MOST_SAME * max(1, rows_dev // tile_side)
    devices = lax.axis_size("row")
    parent = child_rows[:, 0]
    grouping = parent * tile_side // max(rows_dev, tile_side)
    sequence = jnp.arange(tile_total, dtype=jnp.int32)
    earlier = (
        (grouping[:, None] == grouping[None, :])
        & (sequence[None, :] < sequence[:, None])
        & selected[None, :]
    )
    slot_ids = jnp.sum(earlier.astype(jnp.int32), axis=1)
    offsets = (
        parent[:, None] * tile_side + jnp.arange(per_tile, dtype=jnp.int32)[None, :] * piece_rows
    )
    targets = jnp.where(selected[:, None], offsets // rows_dev, devices)
    local_ids = offsets % rows_dev // piece_rows
    slot_grid = jnp.broadcast_to(slot_ids[:, None], targets.shape)
    pieces = child_tiles.reshape(tile_total, per_tile, piece_rows, tile_side)
    outgoing = (
        jnp.zeros((devices, capacity, piece_rows, tile_side), child_tiles.dtype)
        .at[targets, slot_grid]
        .set(pieces, mode="drop")
    )
    position = local_ids * tile_rows + child_cols[:, None]
    labels = (
        jnp.full((devices, capacity), -1, jnp.int32)
        .at[targets, slot_grid]
        .set(position, mode="drop")
    )
    return (outgoing, labels)


def place_pieces(arrived, arrived_ids, rows_dev, order):
    piece_rows = arrived.shape[2]
    tile_side = arrived.shape[3]
    tile_rows = order // tile_side
    blocks_dev = rows_dev // piece_rows
    count = arrived.shape[0] * arrived.shape[1]
    selector = (
        arrived_ids.reshape(-1, 1) == jnp.arange(blocks_dev * tile_rows, dtype=jnp.int32)[None, :]
    ).astype(arrived.dtype)
    selector = selector.reshape(count, blocks_dev, tile_rows)
    flattened = arrived.reshape(count, piece_rows, tile_side)
    assembled_part = jnp.einsum(
        "nqc,nsw->qscw", selector, flattened, preferred_element_type=jnp.float32
    )
    return assembled_part.reshape(rows_dev, order)


def local_small(frontal, child_tiles, child_rows, child_cols, gather):
    rows_dev = frontal.shape[0]
    order = frontal.shape[1]
    tile_side = child_tiles.shape[1]
    first_row = lax.axis_index("row") * rows_dev
    current = frontal
    everything = jnp.ones(child_cols.shape, dtype=bool)
    outgoing, labels = pack_pieces(child_tiles, child_rows, child_cols, everything, rows_dev, order)
    arrived, arrived_ids = (
        lax.all_to_all(outgoing, "row", split_axis=0, concat_axis=0, tiled=True),
        lax.all_to_all(labels, "row", split_axis=0, concat_axis=0, tiled=True),
    )
    current = current + place_pieces(arrived, arrived_ids, rows_dev, order)
    leading = gather(current[:, : 2 * tile_side], "row")
    first_all = factor_rows(leading[:, :tile_side], leading[:tile_side, :tile_side], 0)
    second_block = leading[:, tile_side:] - jnp.dot(
        first_all, first_all[tile_side : 2 * tile_side].T, precision=highest
    )
    second_all = factor_rows(second_block, second_block[tile_side : 2 * tile_side], tile_side)
    for panel_index, panel_all in enumerate((first_all, second_all)):
        low_edge = panel_index * tile_side
        panel_own = lax.dynamic_slice_in_dim(panel_all, first_row, rows_dev, 0)
        update = jnp.dot(panel_own, panel_all.T, precision=highest)
        current = apply_panel(current, panel_own, update, low_edge)
    return current


def local(frontal, child_tiles, child_rows, child_cols):
    rows, order = frontal.shape
    side = child_tiles.shape[1]
    devices = lax.axis_size("row")
    wide = rows >= 2 * side and rows % side == 0 and MOST_SAME * rows // side > FIRST + SECOND
    if wide and order == devices * rows and devices % 4 == 0 and devices >= 16 and lax.axis_size("groups") == 2:
        return local_fast(frontal, child_tiles, child_rows, child_cols)
    return local_small(frontal, child_tiles, child_rows, child_cols, gather_rows)


def solution(mesh):
    return jax.shard_map(
        local,
        mesh=mesh,
        in_specs=(
            P(("groups", "row"), None),
            P(("groups", "row"), None, None),
            P(("groups", "row"), None),
            P(("groups", "row")),
        ),
        out_specs=P(("groups", "row"), None),
        check_vma=False,
    )
```
